128 devices in a mesh: cells: 128 (over x, y, z, core).
Axes of the slice: x: 4, y: 4, z: 4, core: 2. Of those that a mesh axis runs over, the one named last changes fastest.
Arguments:
- state_deviation: bfloat16 [540, 262144], P(None, 'cells'), may hold values from -6 to 6
- forcing: bfloat16 [90, 262144], P(None, 'cells'), may hold values from -6 to 6
- trajectory: bfloat16 [540, 65536], P(None, 'cells'), may hold values from -6 to 6
- w_in: bfloat16 [540, 256], replicated, may hold values from -0.25 to 0.25
- w_hidden: bfloat16 [2, 256, 256], replicated, may hold values from -0.375 to 0.375
- w_out: bfloat16 [256, 90], replicated, may hold values from -0.375 to 0.375
- biases: float32 [3, 256], replicated, may hold values from -3 to 3
- fine_order: int32 [128, 2048], P('cells'), may hold values from 0 to 2047, each once within a row
- group_parent: int32 [128, 512], P('cells'), may hold values from 0 to 65535, as said below
- daylit_counts: int32 [128], replicated, may hold values from 0 to 512, as said below
- sun_rank: int32 [128, 512], P('cells'), may hold values from 0 to 511, each once within a row
- adjacent_source_slots: int32 [6, 262144], P(None, 'cells'), may hold values from 0 to 2559, as said below
- outgoing_local_lists: int32 [128, 2, 256], P('cells'), may hold values from 0 to 2047, as said below
Outputs:
- tl_temperature: float32 [90, 262144], P(None, 'cells')
- forcing_sensitivity_vector: bfloat16 [540, 262144], P(None, 'cells')
The draws below stay inside these ranges and needn't reach their ends.
Inputs may be any that keep to these rules, and one draw needn't show every extreme that they name: `fine_order`: each row is a permutation of the fine cells of one device. `group_parent`: every radiation column is the parent of exactly one group; at most 8 groups of one device have their columns on any one device, and in every draw 8 do for every device. `daylit_counts`: the counts of device i and of device i xor (half the number of devices) sum to 512 or less, to exactly 512 for some pair. `sun_rank`: each row is a permutation. `adjacent_source_slots`: entries below 2048 are own cells, 2048 to 2303 the cells received from the device below, the rest those from the device above; within one of the six rows, the cells of one device never name the same entry twice. `outgoing_local_lists`: each list holds 256 distinct local cells.
All inputs are finite; a program needn't handle non-finite values.
Results may differ from the reference program's by a relative error of at most 0.01.
Values may be sent and summed in bfloat16 or wider, within the bound.
No kernel may reach another device: no remote copies, remote signals or barrier semaphores. Data moves between devices by JAX's collectives and lax.ppermute only.
A program may use at most 128 MiB of HBM per device.

```python
import jax
import jax.numpy as jnp
from jax import lax

LEV = 90
FEAT = 540
HID = 256
C_DEV = 512
F_DEV = 2048
ROW = 255
HS = 256
SUBSTEPS = 3
NC = 65536
NF = 262144
N_CELLS = 128


def permute_rows(base_key, length):
    return jax.vmap(lambda subkey: jax.random.permutation(subkey, length))(jax.random.split(base_key, N_CELLS))


def grid_layout(key):
    subkeys = jax.random.split(key, 3)
    storage = permute_rows(subkeys[0], F_DEV)
    down_order = permute_rows(subkeys[1], HS)
    up_order = permute_rows(subkeys[2], HS)
    device_rows = jnp.arange(N_CELLS, dtype=jnp.int32)[:, None]
    sends_down = jnp.take_along_axis(storage, down_order, axis=1)
    sends_up = jnp.take_along_axis(storage, F_DEV - HS + up_order, axis=1)
    outgoing_local_lists = jnp.stack([sends_down, sends_up], axis=1)
    counting = jnp.broadcast_to(jnp.arange(HS, dtype=jnp.int32), (N_CELLS, HS))
    down_pos = jnp.zeros((N_CELLS, HS), jnp.int32).at[device_rows, down_order].set(counting)
    up_pos = jnp.zeros((N_CELLS, HS), jnp.int32).at[device_rows, up_order].set(counting)
    logical = jnp.arange(F_DEV, dtype=jnp.int32)[None, :] + device_rows * F_DEV
    offsets = jnp.array([1, -1, ROW, -ROW - 1, ROW + 1, 1 - ROW], dtype=jnp.int32)
    target = (logical[None] + offsets[:, None, None]) % (N_CELLS * F_DEV)
    owner_device = target // F_DEV
    owner_spot = target % F_DEV
    device_grid = jnp.broadcast_to(device_rows[None], target.shape)
    same_device = owner_device == device_grid
    from_below = owner_device == (device_grid - 1) % N_CELLS
    local_index = jnp.take_along_axis(jnp.broadcast_to(storage[None], target.shape), owner_spot, axis=2)
    below_table = jnp.broadcast_to(jnp.roll(up_pos, 1, axis=0)[None], (6, N_CELLS, HS))
    above_table = jnp.broadcast_to(jnp.roll(down_pos, -1, axis=0)[None], (6, N_CELLS, HS))
    below_index = F_DEV + jnp.take_along_axis(below_table, jnp.clip(owner_spot - (F_DEV - HS), 0, HS - 1), axis=2)
    above_index = F_DEV + HS + jnp.take_along_axis(above_table, jnp.clip(owner_spot, 0, HS - 1), axis=2)
    extended = jnp.where(same_device, local_index, jnp.where(from_below, below_index, above_index))
    link_rows = jnp.broadcast_to(jnp.arange(6, dtype=jnp.int32)[:, None, None], target.shape)
    link_table = jnp.zeros((6, N_CELLS, F_DEV), jnp.int32).at[link_rows, device_grid, jnp.broadcast_to(storage[None], target.shape)].set(extended)
    return (link_table.reshape(6, N_CELLS * F_DEV).astype(jnp.int32), outgoing_local_lists.astype(jnp.int32))


def draw_adjacent_source_slots(key, part):
    shared = grid_layout(key)
    return shared[0]


def draw_outgoing_local_lists(key, part):
    shared = grid_layout(key)
    return shared[1]


def draw_group_parent(key, part):
    key = jax.random.fold_in(key, 11)
    subkeys = jax.random.split(key, 4)
    per_pair = C_DEV // N_CELLS
    half_cells = N_CELLS // 2
    extra = jax.random.randint(subkeys[0], (half_cells,), 0, per_pair + 1)
    forced = jax.random.randint(subkeys[1], (), 0, half_cells)
    extra = jnp.where(jnp.arange(half_cells) == forced, per_pair, extra)
    offsets = jnp.stack([extra, -extra], axis=1).reshape(N_CELLS)
    device_rows = jnp.arange(N_CELLS, dtype=jnp.int32)[:, None]
    counts = per_pair + offsets[(jnp.arange(N_CELLS, dtype=jnp.int32)[None, :] - device_rows) % N_CELLS]
    finish = jnp.cumsum(counts, axis=1)
    starts = finish - counts
    arrivals = jnp.cumsum(counts, axis=0) - counts
    position = jnp.arange(C_DEV, dtype=jnp.int32)
    target_device = jnp.sum((finish[:, None, :] <= position[None, :, None]).astype(jnp.int32), axis=2)
    within = position[None, :] - jnp.take_along_axis(starts, target_device, axis=1)
    incoming = jnp.take_along_axis(arrivals, target_device, axis=1) + within
    coarse_perm = permute_rows(subkeys[2], C_DEV)
    coarse_local = coarse_perm[target_device, incoming]
    group_perm = permute_rows(subkeys[3], C_DEV)
    values = target_device * C_DEV + coarse_local
    result = jnp.zeros((N_CELLS, C_DEV), jnp.int32).at[jnp.broadcast_to(device_rows, (N_CELLS, C_DEV)), group_perm].set(values)
    return result.astype(jnp.int32)


def draw_daylit_counts(key, part):
    key = jax.random.fold_in(key, 23)
    subkeys = jax.random.split(key, 3)
    half_cells = N_CELLS // 2
    lower_half = jax.random.randint(subkeys[0], (half_cells,), 0, C_DEV + 1)
    slack = jax.random.randint(subkeys[1], (half_cells,), 0, C_DEV // 8 + 1)
    forced = jax.random.randint(subkeys[2], (), 0, half_cells)
    chosen = jnp.arange(half_cells) == forced
    lower_half = jnp.where(chosen, C_DEV, lower_half)
    slack = jnp.where(chosen, 0, slack)
    upper_half = jnp.maximum(C_DEV - lower_half - slack, 0)
    return jnp.concatenate([lower_half, upper_half]).astype(jnp.int32)


def block_scale(key, extent, cuts, smallest, largest):
    def one(dim, blocks):
        heights = jax.random.uniform(jax.random.fold_in(jax.random.fold_in(key, 6), dim), (blocks,), jnp.float32, smallest / len(cuts), largest / len(cuts))
        return jnp.repeat(jnp.exp(heights), extent[dim] // blocks).reshape((-1,) + (1,) * (len(extent) - dim - 1))

    loudness = one(*cuts[0])
    for cut in cuts[1:]:
        loudness = loudness * one(*cut)
    return loudness


def scatter_about(own_key, extent, spread, most, cuts=(), kind=jnp.bfloat16):
    drawn = spread * jax.random.normal(own_key, extent, jnp.float32)
    if cuts:
        drawn = drawn * block_scale(own_key, extent, cuts, -0.22, 0.18)
    return jnp.clip(drawn, -most, most).astype(kind)


def setup_inputs(seed: int = 0) -> dict:
    key_of = jax.random.split(jax.random.key(seed), 14)
    return {
        "state_deviation": scatter_about(key_of[0], (FEAT, NF), 1.0, 6.0, ((1, 128),)),
        "forcing": scatter_about(key_of[1], (LEV, NF), 1.0, 6.0, ((1, 128),)),
        "trajectory": scatter_about(key_of[2], (FEAT, NC), 1.0, 6.0, ((1, 128),)),
        "w_in": scatter_about(key_of[3], (FEAT, HID), FEAT ** -0.5, 0.25),
        "w_hidden": scatter_about(key_of[4], (2, HID, HID), HID ** -0.5, 0.375),
        "w_out": scatter_about(key_of[5], (HID, LEV), HID ** -0.5, 0.375),
        "biases": scatter_about(key_of[6], (3, HID), 0.5, 3.0, (), jnp.float32),
        "fine_order": jax.vmap(lambda own: jax.random.permutation(own, F_DEV))(jax.random.split(key_of[7], N_CELLS)).reshape((N_CELLS, F_DEV)).astype(jnp.int32),
        "group_parent": draw_group_parent(jax.random.fold_in(key_of[13], 71), 0),
        "daylit_counts": draw_daylit_counts(jax.random.fold_in(key_of[13], 71), 0),
        "sun_rank": jax.vmap(lambda own: jax.random.permutation(own, C_DEV))(jax.random.split(key_of[10], N_CELLS)).reshape((N_CELLS, C_DEV)).astype(jnp.int32),
        "adjacent_source_slots": draw_adjacent_source_slots(jax.random.fold_in(key_of[13], 71), 0),
        "outgoing_local_lists": draw_outgoing_local_lists(jax.random.fold_in(key_of[13], 71), 0),
    }


spreading_coefficient = 0.125

def contract(weight, operand):
    return lax.dot_general(weight, operand, (((0,), (0,)), ((), ())), preferred_element_type=jnp.float32)

def network_pass(inputs, daylit, tangent, adjoint, w_in, w_hidden, w_out, biases):
    act_one = jnp.tanh(contract(w_in, inputs) + biases[0][:, None])
    act_two = jnp.tanh(contract(w_hidden[0], act_one.astype(jnp.bfloat16)) + biases[1][:, None])
    act_three = jnp.tanh(contract(w_hidden[1], act_two.astype(jnp.bfloat16)) + biases[2][:, None])
    slope_one = 1.0 - act_one * act_one
    slope_two = 1.0 - act_two * act_two
    slope_three = 1.0 - act_three * act_three
    forward = (slope_one * contract(w_in, tangent)).astype(jnp.bfloat16)
    forward = (slope_two * contract(w_hidden[0], forward)).astype(jnp.bfloat16)
    forward = (slope_three * contract(w_hidden[1], forward)).astype(jnp.bfloat16)
    heating = (daylit[None, :] * contract(w_out, forward)).astype(jnp.bfloat16)
    backward = (slope_three * jnp.dot(w_out, adjoint, preferred_element_type=jnp.float32)).astype(jnp.bfloat16)
    backward = (slope_two * jnp.dot(w_hidden[1], backward, preferred_element_type=jnp.float32)).astype(jnp.bfloat16)
    backward = (slope_one * jnp.dot(w_hidden[0], backward, preferred_element_type=jnp.float32)).astype(jnp.bfloat16)
    sensitivity = jnp.dot(w_in, backward, preferred_element_type=jnp.float32).astype(jnp.bfloat16)
    return (heating, sensitivity)

def group_children(fine_order):
    cell_count = fine_order.shape[1]
    device_rows = jnp.arange(fine_order.shape[0], dtype=jnp.int32)[:, None]
    counting = jnp.broadcast_to(jnp.arange(cell_count, dtype=jnp.int32), fine_order.shape)
    inverse = jnp.zeros(fine_order.shape, jnp.int32).at[device_rows, fine_order].set(counting)
    return inverse.reshape(fine_order.shape[0], cell_count // 4, 4)

def group_sums(values, children):
    overall_reduction_sum = jnp.zeros((values.shape[0], values.shape[1], children.shape[1]), jnp.float32)
    for member in range(4):
        overall_reduction_sum = overall_reduction_sum + jnp.take_along_axis(values, children[None, :, :, member], axis=2).astype(jnp.float32)
    return overall_reduction_sum

def spreading_increment(profile, adjacent_source_slots, outgoing_local_lists):
    blocks = profile.reshape(profile.shape[0], N_CELLS, F_DEV)
    from_below = jnp.take_along_axis(jnp.roll(blocks, 1, axis=1), jnp.roll(outgoing_local_lists[:, 1, :], 1, axis=0)[None], axis=2)
    from_above = jnp.take_along_axis(jnp.roll(blocks, -1, axis=1), jnp.roll(outgoing_local_lists[:, 0, :], -1, axis=0)[None], axis=2)
    extended = jnp.concatenate([blocks, from_below, from_above], axis=2)
    link_table = adjacent_source_slots.reshape(6, N_CELLS, F_DEV)
    overall_reduction_sum = jnp.zeros_like(blocks)
    for link_index in range(6):
        overall_reduction_sum = overall_reduction_sum + jnp.take_along_axis(extended, link_table[link_index][None], axis=2)
    return (blocks + spreading_coefficient * (overall_reduction_sum - 6.0 * blocks)).reshape(profile.shape)

def reference(state_deviation, forcing, trajectory, w_in, w_hidden, w_out, biases, fine_order, group_parent, daylit_counts, sun_rank, adjacent_source_slots, outgoing_local_lists):
    features = state_deviation.shape[0]
    column_layer_count = forcing.shape[0]
    children = group_children(fine_order)
    parents = group_parent.reshape(-1)
    mean_pert = (group_sums(state_deviation.reshape(features, N_CELLS, F_DEV), children) * 0.25).astype(jnp.bfloat16)
    tangent_in = jnp.zeros((features, NC), jnp.bfloat16).at[:, parents].set(mean_pert.reshape(features, NC))
    daylit = (sun_rank < daylit_counts[:, None]).astype(jnp.float32).reshape(NC)
    adjoint = forcing.astype(jnp.float32)
    heat_back = adjoint
    for substep in range(SUBSTEPS):
        _, pullback = jax.vjp(lambda profile: spreading_increment(profile, adjacent_source_slots, outgoing_local_lists), adjoint)
        adjoint = pullback(adjoint)[0]
        if substep + 1 < SUBSTEPS:
            heat_back = heat_back + adjoint
    back_sum = group_sums(heat_back.reshape(column_layer_count, N_CELLS, F_DEV), children).astype(jnp.bfloat16)
    back_coarse = jnp.zeros((column_layer_count, NC), jnp.bfloat16).at[:, parents].set(back_sum.reshape(column_layer_count, NC))
    back_in = (daylit[None, :] * back_coarse.astype(jnp.float32)).astype(jnp.bfloat16)
    heating, sensitivity = network_pass(trajectory, daylit, tangent_in, back_in, w_in, w_hidden, w_out, biases)
    owner_group = (fine_order // 4 + jnp.arange(N_CELLS, dtype=jnp.int32)[:, None] * C_DEV).reshape(-1)
    coarse_of = parents[owner_group]
    warming_detailed_sites = heating[:, coarse_of].astype(jnp.float32)
    atmospheric_warmth = state_deviation[:column_layer_count].astype(jnp.float32)
    for substep in range(SUBSTEPS):
        atmospheric_warmth = spreading_increment(atmospheric_warmth, adjacent_source_slots, outgoing_local_lists) + warming_detailed_sites
    forcing_sensitivity_vector = sensitivity[:, coarse_of].astype(jnp.float32) * 0.25
    forcing_sensitivity_vector = forcing_sensitivity_vector.at[:column_layer_count].add(adjoint)
    return (atmospheric_warmth, forcing_sensitivity_vector.astype(jnp.bfloat16))
```

```python
import jax
import jax.numpy as jnp
from jax import lax
from jax.experimental import pallas as pl
from jax.experimental.pallas import tpu as pltpu
from jax.sharding import PartitionSpec as P

LEV, FEAT, HID = 90, 540, 256
COLS, CELLS, HALO = 512, 2048, 256
EXT = CELLS + 2 * HALO
DEVS, CAP = 128, 8
SLOTS = DEVS * CAP
KEEP, SPREAD = 0.25, 0.125

f32, bf16, i32 = jnp.float32, jnp.bfloat16, jnp.int32
NN = (((1,), (0,)), ((), ()))
NT = (((1,), (1,)), ((), ()))
TN = (((0,), (0,)), ((), ()))
VMEM = pl.BlockSpec(memory_space=pltpu.VMEM)
SMEM = pl.BlockSpec(memory_space=pltpu.SMEM)


def dot(a, b, dims):
    return lax.dot_general(a, b, dims, preferred_element_type=f32)


def shape(dims, dtype):
    return jax.ShapeDtypeStruct(dims, dtype)


def kernel(body, outs, args, specs=None, scratch=(), limit=24, flops=0, name=None):
    bytes_accessed = sum(a.size * a.dtype.itemsize for a in args)
    bytes_accessed += sum(o.size * o.dtype.itemsize for o in outs)
    return pl.pallas_call(
        body,
        out_shape=outs,
        in_specs=specs or [VMEM] * len(args),
        out_specs=tuple(VMEM for _ in outs),
        scratch_shapes=list(scratch),
        compiler_params=pltpu.CompilerParams(vmem_limit_bytes=limit * 1024 * 1024),
        cost_estimate=pl.CostEstimate(
            flops=flops, bytes_accessed=bytes_accessed, transcendentals=0
        ),
        name=name,
    )(*args)


def row_iota(rows, columns):
    return lax.broadcasted_iota(i32, (rows, columns), 0)


def lane_iota(rows, columns):
    return lax.broadcasted_iota(i32, (rows, columns), 1)


def onehot(mask):
    return jnp.where(mask, 1.0, 0.0).astype(bf16)


def to_column(row):
    return jnp.broadcast_to(row, (128, row.shape[1])).T[:, :1]


def chunk(i, size):
    return pl.ds(pl.multiple_of(i * size, size), size)


def route_kernel(parent_ref, request_ref, slot_ref):
    parents = parent_ref[...]
    target = parents >> 9
    column = (parents & (COLS - 1)) + 1
    target_column = to_column(target.astype(f32))
    same = (target_column == target.astype(f32)) & (row_iota(COLS, COLS) < lane_iota(COLS, COLS))
    rank = jnp.sum(jnp.where(same, 1.0, 0.0), axis=0, keepdims=True).astype(i32)
    slot_ref[...] = target * CAP + rank
    owners = onehot(row_iota(DEVS, COLS) == target)
    ranked = row_iota(DEVS, COLS) == rank
    high = jnp.where(ranked, (column >> 4).astype(f32), 0.0).astype(bf16)
    low = jnp.where(ranked, (column & 15).astype(f32), 0.0).astype(bf16)
    request = dot(owners, high, NT) * 16.0 + dot(owners, low, NT)
    request_ref[...] = request.reshape(DEVS, 1, 128)


def build_kernel(
    slots_ref, forcing_ref, state_ref, lists_ref, traj_ref, w_in_ref, bias_ref,
    links_ref, border_ref, u_ref, part_ref, up_ref, down_ref,
):
    slots = slots_ref[...]
    high = slots >> 8
    low = slots & 255
    times = jnp.zeros((6, CELLS), f32)
    for k in range(6):
        times = times + jnp.where(slots == slots[k : k + 1, :], 1.0, 0.0)
    times = times.astype(bf16)
    forcing = forcing_ref[...]

    def block(jb):
        here = jnp.where(high == jb, low, -1).astype(f32).astype(bf16)
        rows = chunk(jb, 256)
        for c in range(8):
            sl = slice(c * 256, (c + 1) * 256)
            place = row_iota(256, 256).astype(f32).astype(bf16)
            count = jnp.zeros((256, 256), bf16)
            for k in range(6):
                count = jnp.where(here[k : k + 1, sl] == place, times[k : k + 1, sl], count)
            links_ref[rows, sl] = count
        return SPREAD * dot(forcing, links_ref[rows, :], NT)

    def own(jb, _):
        cells = chunk(jb, 256)
        part_ref[:, cells] = KEEP * forcing_ref[:, cells].astype(f32) + block(jb)
        return 0

    lax.fori_loop(0, 8, own, 0)
    down_ref[0] = block(8).astype(bf16)
    up_ref[0] = block(9).astype(bf16)

    for b in range(8):
        sl = slice(b * 256, (b + 1) * 256)
        for side in range(2):
            border_ref[sl, side * 256 : (side + 1) * 256] = onehot(
                row_iota(256, 256) + b * 256 == lists_ref[side : side + 1, :]
            )
    border = dot(state_ref[:LEV, :], border_ref[...], NN)
    down_ref[1] = border[:, :HALO].astype(bf16)
    up_ref[1] = border[:, HALO:].astype(bf16)

    z = dot(traj_ref[...], w_in_ref[...], TN) + bias_ref[0:1, :]
    decay = jnp.exp(-2.0 * jnp.minimum(jnp.abs(z), 30.0))
    u_ref[...] = jnp.where(z < 0.0, -decay, decay).astype(bf16)


def answer_kernel(request_ref, u_ref, rank_ref, count_ref, answer_ref, left_ref, right_ref):
    daylit = rank_ref[...] < count_ref[0]
    number = jnp.where(daylit, lane_iota(1, COLS) + 1, -1).astype(f32)
    request = request_ref[...].reshape(DEVS, 128)
    for k in range(CAP):
        chosen = onehot(request[:, k : k + 1] == number)
        rows = dot(chosen, u_ref[...], NN)
        left_ref[pl.ds(k, DEVS, stride=CAP), :] = rows[:, :128]
        right_ref[pl.ds(k, DEVS, stride=CAP), :] = rows[:, 128:]
    answer_ref[:, :128] = left_ref[...].astype(bf16)
    answer_ref[:, 128:] = right_ref[...].astype(bf16)


def adjoint_step(adjoint, links_ref, part_ref, up_ref, down_ref, scratch_ref):
    scratch_ref[...] = adjoint
    rounded = adjoint.astype(bf16)

    def own(jb, _):
        cells = chunk(jb, 256)
        part_ref[:, cells] = KEEP * scratch_ref[:, cells] + SPREAD * dot(
            rounded, links_ref[cells, :], NT
        )
        return 0

    lax.fori_loop(0, 8, own, 0)
    down_ref[0] = (SPREAD * dot(rounded, links_ref[CELLS : CELLS + HALO, :], NT)).astype(bf16)
    up_ref[0] = (SPREAD * dot(rounded, links_ref[CELLS + HALO :, :], NT)).astype(bf16)


def second_kernel(
    part_ref, below_ref, above_ref, links_ref, border_ref, state_ref, forcing_ref,
    next_ref, up_ref, down_ref, heat_back_ref, first_ref, scratch_ref,
):
    adjoint = (
        part_ref[...]
        + dot(below_ref[0], border_ref[:, :HALO], NT)
        + dot(above_ref[0], border_ref[:, HALO:], NT)
    )
    heat_back_ref[...] = forcing_ref[...].astype(f32) + adjoint
    adjoint_step(adjoint, links_ref, next_ref, up_ref, down_ref, scratch_ref)

    def ahead(c, _):
        cells = chunk(c, 256)
        total = dot(state_ref[:LEV, :], links_ref[:CELLS, cells], NN)
        total = total + dot(below_ref[1], links_ref[CELLS : CELLS + HALO, cells], NN)
        total = total + dot(above_ref[1], links_ref[CELLS + HALO :, cells], NN)
        first_ref[:, cells] = KEEP * state_ref[:LEV, cells].astype(f32) + SPREAD * total
        return 0

    lax.fori_loop(0, 8, ahead, 0)


def group_kernel(order_ref, state_ref, w_in_ref, groups_ref, drive_ref):
    group = order_ref[...] >> 2
    for c in range(8):
        sl = slice(c * 256, (c + 1) * 256)
        groups_ref[:, sl] = onehot(row_iota(COLS, 256) == group[:, sl])
    mean = (0.25 * dot(state_ref[...], groups_ref[...], NT)).astype(bf16)
    drive_ref[...] = dot(w_in_ref[...], mean, TN)


def third_kernel(
    part_ref, below_ref, above_ref, links_ref, border_ref, heat_back_ref, groups_ref,
    next_ref, up_ref, down_ref, back_ref, scratch_ref,
):
    adjoint = (
        part_ref[...]
        + dot(below_ref[0], border_ref[:, :HALO], NT)
        + dot(above_ref[0], border_ref[:, HALO:], NT)
    )
    total = heat_back_ref[...] + adjoint
    back_ref[...] = dot(total.astype(bf16), groups_ref[...], NT).astype(bf16)
    adjoint_step(adjoint, links_ref, next_ref, up_ref, down_ref, scratch_ref)


def network_kernel(
    answer_ref, slot_ref, drive_ref, first_ref, groups_ref, border_ref, w_hidden_ref, w_out_ref,
    bias_ref, heat_ref, temp_ref, up_ref, down_ref, slope_ref,
):
    chosen = onehot(row_iota(SLOTS, COLS) == slot_ref[...])
    u = dot(answer_ref[...], chosen, TN)
    size = jnp.abs(u)
    inverse = 1.0 / (1.0 + size)
    act = jnp.where(u < 0.0, size - 1.0, 1.0 - size) * inverse
    slope = 4.0 * size * inverse * inverse
    slope_ref[0] = slope
    tangent = (slope * drive_ref[...]).astype(bf16)
    for layer in range(2):
        weight = w_hidden_ref[layer]
        bias = to_column(bias_ref[layer + 1 : layer + 2, :])
        act = jnp.tanh(dot(weight, act.astype(bf16), TN) + bias)
        slope = 1.0 - act * act
        slope_ref[layer + 1] = slope
        tangent = (slope * dot(weight, tangent, TN)).astype(bf16)
    heating = dot(w_out_ref[...], tangent, TN).astype(bf16)
    heat = dot(heating, groups_ref[...], NN)
    heat_ref[...] = heat
    temp = first_ref[...] + heat
    temp_ref[...] = temp
    border = dot(temp.astype(bf16), border_ref[...], NN)
    down_ref[...] = border[:, :HALO].astype(bf16)
    up_ref[...] = border[:, HALO:].astype(bf16)


def inner_kernel(temp_ref, heat_ref, links_ref, part_ref):
    rounded = temp_ref[...].astype(bf16)

    def own(c, _):
        cells = chunk(c, 256)
        total = dot(rounded, links_ref[:CELLS, cells], NN)
        part_ref[:, cells] = KEEP * temp_ref[:, cells] + heat_ref[:, cells] + SPREAD * total
        return 0

    lax.fori_loop(0, 8, own, 0)


def outer(part_ref, below_ref, above_ref, links_ref, temp_ref):
    def halo(c, _):
        cells = chunk(c, 256)
        total = dot(below_ref[...], links_ref[CELLS : CELLS + HALO, cells], NN)
        total = total + dot(above_ref[...], links_ref[CELLS + HALO :, cells], NN)
        temp_ref[:, cells] = part_ref[:, cells] + SPREAD * total
        return 0

    lax.fori_loop(0, 8, halo, 0)


def outer_kernel(
    part_ref, below_ref, above_ref, links_ref, border_ref, temp_ref, up_ref, down_ref
):
    outer(part_ref, below_ref, above_ref, links_ref, temp_ref)
    border = dot(temp_ref[...].astype(bf16), border_ref[...], NN)
    down_ref[...] = border[:, :HALO].astype(bf16)
    up_ref[...] = border[:, HALO:].astype(bf16)


def last_kernel(part_ref, below_ref, above_ref, links_ref, temp_ref):
    outer(part_ref, below_ref, above_ref, links_ref, temp_ref)


def sensitivity_kernel(
    back_ref, slope_ref, w_in_ref, w_hidden_ref, w_out_ref, groups_ref,
    part_ref, below_ref, above_ref, border_ref, out_ref,
):
    back = (slope_ref[2] * dot(w_out_ref[...], back_ref[...], NN)).astype(bf16)
    back = (slope_ref[1] * dot(w_hidden_ref[1], back, NN)).astype(bf16)
    back = (slope_ref[0] * dot(w_hidden_ref[0], back, NN)).astype(bf16)
    sens = (0.25 * dot(w_in_ref[...], back, NN)).astype(bf16)

    def spread(c, _):
        cells = chunk(c, 256)
        fine = dot(sens, groups_ref[:, cells], NN)
        adjoint = (
            part_ref[:, cells]
            + dot(below_ref[0], border_ref[cells, :HALO], NT)
            + dot(above_ref[0], border_ref[cells, HALO:], NT)
        )
        out_ref[:, cells] = fine.astype(bf16)
        out_ref[:LEV, cells] = (fine[:LEV] + adjoint).astype(bf16)
        return 0

    lax.fori_loop(0, 8, spread, 0)


def local(
    state_deviation, forcing, trajectory, w_in, w_hidden, w_out, biases, fine_order, group_parent,
    daylit_counts, sun_rank, adjacent_source_slots, outgoing_local_lists,
):
    up_pairs = [(i, (i + 1) % DEVS) for i in range(DEVS)]
    down_pairs = [(j, i) for i, j in up_pairs]

    def swap(up, down):
        below = lax.ppermute(up, "cells", up_pairs)
        above = lax.ppermute(down, "cells", down_pairs)
        return below, above

    count = lax.dynamic_slice(daylit_counts, (lax.axis_index("cells"),), (1,))
    lists = outgoing_local_lists[0]

    request, slot = kernel(
        route_kernel,
        (shape((DEVS, 1, 128), f32), shape((1, COLS), i32)),
        (group_parent,),
        flops=10**7,
        name="route",
    )
    asked = lax.all_to_all(request, "cells", 0, 0, tiled=True)

    message = shape((2, LEV, HALO), bf16)
    single = shape((1, LEV, HALO), bf16)
    plain = shape((LEV, HALO), bf16)
    field = shape((LEV, CELLS), f32)
    links, border, u, part, up, down = kernel(
        build_kernel,
        (
            shape((EXT, CELLS), bf16),
            shape((CELLS, 2 * HALO), bf16),
            shape((COLS, HID), bf16),
            field,
            message,
            message,
        ),
        (adjacent_source_slots, forcing, state_deviation, lists, trajectory, w_in, biases),
        flops=3 * 10**9,
        name="build",
    )
    below, above = swap(up, down)
    (answer,) = kernel(
        answer_kernel,
        (shape((SLOTS, HID), bf16),),
        (asked, u, sun_rank, count),
        specs=[VMEM, VMEM, VMEM, SMEM],
        scratch=[pltpu.VMEM((SLOTS, 128), f32)] * 2,
        flops=10**9,
        name="answer",
    )
    got = lax.all_to_all(answer.reshape(DEVS, CAP, HID), "cells", 0, 0, tiled=True)
    got = got.reshape(SLOTS, HID)

    groups, drive = kernel(
        group_kernel,
        (shape((COLS, CELLS), bf16), shape((HID, COLS), f32)),
        (fine_order, state_deviation, w_in),
        flops=2 * 10**9,
        name="group",
    )
    part, up, down, heat_back, first = kernel(
        second_kernel,
        (field, single, single, field, field),
        (part, below, above, links, border, state_deviation, forcing),
        scratch=[pltpu.VMEM((LEV, CELLS), f32)],
        flops=3 * 10**9,
        name="second",
    )
    below, above = swap(up, down)
    part, up, down, back = kernel(
        third_kernel,
        (field, single, single, shape((LEV, COLS), bf16)),
        (part, below, above, links, border, heat_back, groups),
        scratch=[pltpu.VMEM((LEV, CELLS), f32)],
        flops=3 * 10**9,
        name="third",
    )
    below, above = swap(up, down)

    heat, temp, up, down, slope = kernel(
        network_kernel,
        (field, field, plain, plain, shape((3, HID, COLS), f32)),
        (got, slot, drive, first, groups, border, w_hidden, w_out, biases),
        flops=3 * 10**9,
        name="network",
    )
    t_below, t_above = swap(up, down)
    (inner,) = kernel(inner_kernel, (field,), (temp, heat, links), flops=10**9, name="inner")
    (sens,) = kernel(
        sensitivity_kernel,
        (shape((FEAT, CELLS), bf16),),
        (back, slope, w_in, w_hidden, w_out, groups, part, below, above, border),
        flops=2 * 10**9,
        name="sensitivity",
    )
    temp, up, down = kernel(
        outer_kernel,
        (field, plain, plain),
        (inner, t_below, t_above, links, border),
        flops=10**9,
        name="outer",
    )
    t_below, t_above = swap(up, down)
    (inner,) = kernel(inner_kernel, (field,), (temp, heat, links), flops=10**9, name="inner")
    (temp,) = kernel(last_kernel, (field,), (inner, t_below, t_above, links), flops=10**9, name="last")
    return temp, sens


def solution(mesh):
    return jax.shard_map(
        local,
        mesh=mesh,
        in_specs=(
            P(None, "cells"),
            P(None, "cells"),
            P(None, "cells"),
            P(),
            P(),
            P(),
            P(),
            P("cells", None),
            P("cells", None),
            P(),
            P("cells", None),
            P(None, "cells"),
            P("cells", None, None),
        ),
        out_specs=(P(None, "cells"), P(None, "cells")),
        check_vma=False,
    )
```

```python
import jax
import jax.numpy as jnp
from jax import lax
from jax.experimental import pallas as pl
from jax.experimental.pallas import tpu as pltpu
from jax.sharding import PartitionSpec as P

LEV, FEAT, HID = 90, 540, 256
COLS, CELLS, HALO = 512, 2048, 256
EXT = CELLS + 2 * HALO
DEVS, CAP = 128, 8
SLOTS = DEVS * CAP
KEEP, SPREAD = 0.25, 0.125
TOP = 96
PIECE = 512
OWN = CELLS // PIECE

f32, bf16, i32 = jnp.float32, jnp.bfloat16, jnp.int32
NN = (((1,), (0,)), ((), ()))
NT = (((1,), (1,)), ((), ()))
TN = (((0,), (0,)), ((), ()))


def dot(a, b, dims):
    return lax.dot_general(a, b, dims, preferred_element_type=f32)


def shape(dims, dtype):
    return jax.ShapeDtypeStruct(dims, dtype)


class Fetch:
    def __init__(self, source, ref, sems, rows, start):
        self.ref, self.rows, self.copies, self.done = ref, rows, [], set()
        for i in range(ref.shape[0] // rows):
            part = pl.ds(i * rows, rows)
            origin = source.at[pl.ds(start + i * rows, rows)]
            self.copies.append(pltpu.make_async_copy(origin, ref.at[part], sems.at[i]))

    def order(self):
        return [len(self.copies) - 1, *range(len(self.copies) - 1)]

    def __call__(self):
        for i in range(len(self.copies)):
            self.piece(i)
        return self.ref

    def piece(self, i):
        if i not in self.done:
            self.copies[i].wait()
            self.done.add(i)
        return self.ref.at[pl.ds(i * self.rows, self.rows)]


class Store:
    def __init__(self, target, ref, sem):
        self.ref = ref
        self.copy = pltpu.make_async_copy(ref, target, sem)

    def put(self):
        self.copy.start()


def kernel(body, name, args, outs, limit=48, flops=10**9, scratch=(), aliases=None):
    arrays, in_specs, plan, scratches = [], [], [], []
    for arg in args:
        if isinstance(arg, tuple) and arg[0] == "raw":
            arrays.append(pltpu.with_memory_space_constraint(arg[1], pltpu.HBM))
            in_specs.append(pl.BlockSpec(memory_space=pl.ANY))
            plan.append(None)
        elif isinstance(arg, tuple):
            array, rows, piece, *start = arg
            arrays.append(pltpu.with_memory_space_constraint(array, pltpu.HBM))
            in_specs.append(pl.BlockSpec(memory_space=pl.ANY))
            plan.append((piece, start[0] if start else 0))
            scratches.append(pltpu.VMEM((rows,) + array.shape[1:], array.dtype))
            scratches.append(pltpu.SemaphoreType.DMA((rows // piece,)))
        else:
            arrays.append(arg)
            in_specs.append(pl.BlockSpec(memory_space=pltpu.VMEM))
            plan.append(None)
    out_shapes, out_specs = [], []
    for out, far in outs:
        if far == "raw":
            out_shapes.append(pltpu.HBM(out.shape, out.dtype))
            out_specs.append(pl.BlockSpec(memory_space=pl.ANY))
        elif far:
            out_shapes.append(pltpu.HBM(out.shape, out.dtype))
            out_specs.append(pl.BlockSpec(memory_space=pl.ANY))
            scratches.append(pltpu.VMEM(out.shape, out.dtype))
            scratches.append(pltpu.SemaphoreType.DMA)
        else:
            out_shapes.append(out)
            out_specs.append(pl.BlockSpec(memory_space=pltpu.VMEM))

    def wrapped(*refs):
        ins, results = refs[: len(args)], refs[len(args) : len(args) + len(outs)]
        rest = list(refs[len(args) + len(outs) :])
        operands, targets = [], []
        for ref, how in zip(ins, plan):
            if how is None:
                operands.append(ref)
            else:
                place, sems = rest.pop(0), rest.pop(0)
                operands.append(Fetch(ref, place, sems, *how))
        for last in (False, True):
            for o in operands:
                if isinstance(o, Fetch) and (len(o.copies) > 1) == last:
                    for i in o.order():
                        o.copies[i].start()
        for ref, (out, far) in zip(results, outs):
            if far is True:
                targets.append(Store(ref, rest.pop(0), rest.pop(0)))
            else:
                targets.append(ref)
        body(*operands, *targets, *rest)
        for target in targets:
            if isinstance(target, Store):
                target.copy.wait()

    size = sum(a.size * a.dtype.itemsize for a in arrays)
    size += sum(o.size * o.dtype.itemsize for o, _ in outs)
    return pl.pallas_call(
        wrapped,
        out_shape=tuple(out_shapes),
        in_specs=in_specs,
        out_specs=tuple(out_specs),
        scratch_shapes=scratches + list(scratch),
        input_output_aliases=aliases or {},
        compiler_params=pltpu.CompilerParams(vmem_limit_bytes=limit * 1024 * 1024),
        cost_estimate=pl.CostEstimate(flops=flops, bytes_accessed=size, transcendentals=0),
        name=name,
    )(*arrays)


def whole(array):
    return (array, array.shape[0], array.shape[0])


def row_iota(rows, columns):
    return lax.broadcasted_iota(i32, (rows, columns), 0)


def lane_iota(rows, columns):
    return lax.broadcasted_iota(i32, (rows, columns), 1)


def onehot(mask):
    return jnp.where(mask, 1.0, 0.0).astype(bf16)


def to_column(row):
    return jnp.broadcast_to(row, (128, row.shape[1])).T[:, :1]


def chunk(i, size):
    return pl.ds(pl.multiple_of(i * size, size), size)


def route_kernel(parent_ref, request_ref, slot_ref):
    parents = parent_ref[...]
    target = parents >> 9
    column = (parents & (COLS - 1)) + 1
    target_column = to_column(target.astype(f32))
    same = (target_column == target.astype(f32)) & (row_iota(COLS, COLS) < lane_iota(COLS, COLS))
    rank = jnp.sum(jnp.where(same, 1.0, 0.0), axis=0, keepdims=True).astype(i32)
    slot_ref.ref[...] = target * CAP + rank
    slot_ref.put()
    owners = onehot(row_iota(DEVS, COLS) == target)
    ranked = row_iota(DEVS, COLS) == rank
    high = jnp.where(ranked, (column >> 4).astype(f32), 0.0).astype(bf16)
    low = jnp.where(ranked, (column & 15).astype(f32), 0.0).astype(bf16)
    request = dot(owners, high, NT) * 16.0 + dot(owners, low, NT)
    request_ref.ref[...] = request.reshape(DEVS, 1, 128)
    request_ref.put()


def prepare_kernel(
    order_ref, state_ref, w_in_ref, traj_ref, bias_ref, rank_ref, count_ref,
    groups_ref, drive_ref, u_ref, number_ref,
):
    me = lax.axis_index("cells")
    group = order_ref()[...] >> 2
    for c in range(8):
        sl = slice(c * 256, (c + 1) * 256)
        groups_ref.ref[:, sl] = onehot(row_iota(COLS, 256) == group[:, sl])
    groups_ref.put()
    z = dot(traj_ref()[...], w_in_ref()[...], TN) + bias_ref()[0:1, :]
    decay = jnp.exp(-2.0 * jnp.minimum(jnp.abs(z), 30.0))
    u_ref.ref[...] = jnp.where(z < 0.0, -decay, decay).astype(bf16)
    u_ref.put()
    mine = jnp.where(lane_iota(1, DEVS) == me, count_ref()[...], 0).astype(f32)
    daylit = rank_ref()[...].astype(f32) < jnp.sum(mine, axis=1, keepdims=True)
    number_ref.ref[...] = jnp.where(daylit, lane_iota(1, COLS) + 1, -1).astype(f32)
    number_ref.put()
    mean = (0.25 * dot(state_ref()[...], groups_ref.ref[...], NT)).astype(bf16)
    drive_ref.ref[...] = dot(w_in_ref.ref[...], mean, TN)
    drive_ref.put()


def answer_kernel(request_ref, u_ref, number_ref, answer_ref, token_ref, left_ref, right_ref):
    request = request_ref()[...].reshape(DEVS, 128)
    number, u = number_ref()[...], u_ref()
    token_ref[...] = number[:, :128]
    for k in range(CAP):
        chosen = onehot(request[:, k : k + 1] == number)
        rows = dot(chosen, u[...], NN)
        left_ref[pl.ds(k, DEVS, stride=CAP), :] = rows[:, :128]
        right_ref[pl.ds(k, DEVS, stride=CAP), :] = rows[:, 128:]
    answer_ref.ref[:, :128] = left_ref[...].astype(bf16)
    answer_ref.ref[:, 128:] = right_ref[...].astype(bf16)
    answer_ref.put()


def build_kernel(
    slots_ref, lists_ref, forcing_ref, state_ref, token_ref,
    links_ref, border_ref, part_ref, first_ref, second_ref, links, sems,
):
    even = (lax.axis_index("cells") & 1) == 0
    slots = slots_ref()[...]
    high = slots >> 8
    high = jnp.where(even & (high >= 8), 17 - high, high)
    low = slots & 255
    times = jnp.zeros((6, CELLS), f32)
    for k in range(6):
        times = times + jnp.where(slots == slots[k : k + 1, :], 1.0, 0.0)
    times = times.astype(bf16)
    lists = lists_ref()
    near = jnp.where(even, lists[1:2, :], lists[0:1, :])
    far = jnp.where(even, lists[0:1, :], lists[1:2, :])
    forcing = forcing_ref()

    def fill(jb):
        here = jnp.where(high == jb, low, -1).astype(f32).astype(bf16)
        rows = slice(jb * 256, (jb + 1) * 256)
        for c in range(8):
            sl = slice(c * 256, (c + 1) * 256)
            place = row_iota(256, 256).astype(f32).astype(bf16)
            count = jnp.zeros((256, 256), bf16)
            for k in range(6):
                count = jnp.where(here[k : k + 1, sl] == place, times[k : k + 1, sl], count)
            links[rows, sl] = count
        out(jb).start()
        return SPREAD * dot(forcing[...], links[rows, :], NT)

    def out(jb):
        rows = pl.ds(jb * 256, 256)
        return pltpu.make_async_copy(links.at[rows], links_ref.at[rows], sems.at[jb])

    first_ref.ref[0] = fill(8).astype(bf16)
    second_ref.ref[0] = fill(9).astype(bf16)
    state = state_ref()
    for b in range(8):
        sl = slice(b * 256, (b + 1) * 256)
        cell = row_iota(256, 256) + b * 256
        border_ref.ref[sl, :HALO] = onehot(cell == near)
        border_ref.ref[sl, HALO:] = onehot(cell == far)
    border_ref.put()
    border = dot(state[:LEV, :], border_ref.ref[...], NN)
    first_ref.ref[1] = border[:, :HALO].astype(bf16)
    second_ref.ref[1] = border[:, HALO:].astype(bf16)
    first_ref.put()
    second_ref.put()
    for jb in range(8):
        sl = slice(jb * 256, (jb + 1) * 256)
        part_ref.ref[:, sl] = KEEP * forcing[:, sl].astype(f32) + fill(jb)
    part_ref.put()
    for jb in range(10):
        out(jb).wait()


def received(first, second, border):
    return dot(first, border[:, :HALO], NT) + dot(second, border[:, HALO:], NT)


def pull(adjoint, links, wait, part_ref, first_ref, second_ref):
    rounded = adjoint.astype(bf16)
    wait(OWN)
    share = SPREAD * dot(rounded, links[CELLS:, :], NT)
    first_ref[0] = share[:, :HALO].astype(bf16)
    second_ref[0] = share[:, HALO:].astype(bf16)
    for i in range(OWN):
        sl = slice(i * PIECE, (i + 1) * PIECE)
        wait(i)
        part_ref[:, sl] = KEEP * adjoint[:, sl] + SPREAD * dot(rounded, links[sl, :], NT)


def send_border(temp, border, first_ref, second_ref):
    values = dot(temp.astype(bf16), border[...], NN)
    first_ref[1] = values[:, :HALO].astype(bf16)
    second_ref[1] = values[:, HALO:].astype(bf16)


def middle_kernel(
    answer_ref, slot_ref, drive_ref, w_hidden_ref, w_out_ref, bias_ref, first_in, second_in, part_in,
    forcing_ref, state_ref, groups_far, border_far, links_far,
    groups, border, links, heat_ref, temp_ref, slope_ref, part_ref, heat_back_ref, first_ref, second_ref,
    sems,
):
    groups_copy = pltpu.make_async_copy(groups_far, groups, sems.at[5])
    border_copy = pltpu.make_async_copy(border_far, border, sems.at[6])

    def piece(i):
        rows = pl.ds(i * PIECE, PIECE)
        return pltpu.make_async_copy(links_far.at[rows], links.at[rows], sems.at[i])

    groups_copy.start()
    border_copy.start()
    for i in (OWN, *range(OWN)):
        piece(i).start()

    chosen = onehot(row_iota(SLOTS, COLS) == slot_ref()[...])
    u = dot(answer_ref()[...], chosen, TN)
    size = jnp.abs(u)
    inverse = 1.0 / (1.0 + size)
    act = jnp.where(u < 0.0, size - 1.0, 1.0 - size) * inverse
    slope = 4.0 * size * inverse * inverse
    slope_ref[0] = slope
    tangent = (slope * drive_ref()[...]).astype(bf16)
    weights, biases = w_hidden_ref(), bias_ref()
    for layer in range(2):
        weight = weights[layer]
        bias = to_column(biases[layer + 1 : layer + 2, :])
        act = jnp.tanh(dot(weight, act.astype(bf16), TN) + bias)
        slope = 1.0 - act * act
        slope_ref[layer + 1] = slope
        tangent = (slope * dot(weight, tangent, TN)).astype(bf16)
    heating = dot(w_out_ref()[...], tangent, NN).astype(bf16)
    groups_copy.wait()
    heat_ref[...] = dot(heating, groups[...], NN)

    border_copy.wait()
    adjoint = part_in()[...] + received(first_in()[0], second_in()[0], border)
    heat_back_ref[...] = forcing_ref()[...].astype(f32) + adjoint
    pull(adjoint, links, lambda i: piece(i).wait(), part_ref, first_ref, second_ref)
    state = state_ref()
    sides = jnp.concatenate([state[:LEV, :], first_in.ref[1], second_in.ref[1]], axis=1)
    for i in range(OWN):
        sl = slice(i * PIECE, (i + 1) * PIECE)
        temp_ref[:, sl] = (
            KEEP * state[:LEV, sl].astype(f32)
            + heat_ref[:, sl]
            + SPREAD * dot(sides, links[:, sl], NN)
        )
    send_border(temp_ref[...], border, first_ref, second_ref)


def inner(temp_ref, heat_ref, links, part_ref):
    rounded = temp_ref[...].astype(bf16)
    for i in range(OWN):
        sl = slice(i * PIECE, (i + 1) * PIECE)
        part_ref[:, sl] = (
            KEEP * temp_ref[:, sl]
            + heat_ref[:, sl]
            + SPREAD * dot(rounded, links[:CELLS, sl], NN)
        )


def outer(part_ref, first, second, links):
    sides = jnp.concatenate([first, second], axis=1)
    return part_ref[...] + SPREAD * dot(sides, links[CELLS:, :], NN)


def third_kernel(
    first_in, second_in, border, part_in, heat_back_ref, links, ahead_ref,
    part_ref, back_ref, temp_ref, first_ref, second_ref,
):
    adjoint = part_in[...] + received(first_in[0], second_in[0], border)
    back_ref[...] = (heat_back_ref[...] + adjoint).astype(bf16)
    pull(adjoint, links, lambda i: None, part_ref, first_ref, second_ref)
    temp = outer(ahead_ref, first_in[1], second_in[1], links)
    temp_ref[...] = temp
    send_border(temp, border, first_ref, second_ref)


def window_kernel(
    temp_ref, heat_ref, links, slope_ref, back_ref, groups, w_out_ref, w_hidden_ref, w_in_ref,
    sens_far, top_ref, part_ref, low_ref, sem,
):
    inputs = dot(back_ref[...], groups[...], NT).astype(bf16)
    weights = w_hidden_ref()
    back = (slope_ref[2] * dot(w_out_ref()[...], inputs, TN)).astype(bf16)
    back = (slope_ref[1] * dot(weights[1], back, NN)).astype(bf16)
    back = (slope_ref[0] * dot(weights[0], back, NN)).astype(bf16)
    sens = (0.25 * dot(w_in_ref()[...], back, NN)).astype(bf16)
    low_ref[...] = dot(sens[TOP:], groups[...], NN).astype(bf16)
    copy = pltpu.make_async_copy(low_ref, sens_far.at[pl.ds(TOP, FEAT - TOP)], sem)
    copy.start()
    top_ref[...] = dot(sens[:TOP], groups[...], NN)
    inner(temp_ref, heat_ref, links, part_ref)
    copy.wait()


def finish_kernel(
    first_in, second_in, border, part_in, links, ahead_ref, top_in, sens_in,
    sens_far, temp_far, top_ref, sem,
):
    temp_far.ref[...] = outer(ahead_ref, first_in[1], second_in[1], links)
    temp_far.put()
    adjoint = part_in[...] + received(first_in[0], second_in[0], border)
    top_ref[:LEV] = (top_in[:LEV] + adjoint).astype(bf16)
    top_ref[LEV:] = top_in[LEV:].astype(bf16)
    copy = pltpu.make_async_copy(top_ref, sens_far.at[pl.ds(0, TOP)], sem)
    copy.start()
    copy.wait()


def local(
    state_deviation, forcing, trajectory, w_in, w_hidden, w_out, biases, fine_order, group_parent,
    daylit_counts, sun_rank, adjacent_source_slots, outgoing_local_lists,
):
    near_pairs = [(i, i ^ 1) for i in range(DEVS)]
    far_pairs = [(i, (i + 1) % DEVS if i % 2 else (i - 1) % DEVS) for i in range(DEVS)]

    def swap(first, second):
        second = lax.ppermute(second, "cells", far_pairs)
        return lax.ppermute(first, "cells", near_pairs), second

    request, slot = kernel(
        route_kernel,
        "route",
        [group_parent],
        [(shape((DEVS, 1, 128), f32), True), (shape((1, COLS), i32), True)],
        flops=10**7,
    )
    asked = lax.all_to_all(request, "cells", 0, 0, tiled=True)

    side = shape((2, LEV, HALO), bf16)
    field = shape((LEV, CELLS), f32)
    all_links, all_border = shape((EXT, CELLS), bf16), shape((CELLS, 2 * HALO), bf16)
    all_groups = shape((COLS, CELLS), bf16)
    state_rows = (state_deviation, TOP, TOP)

    groups, drive, u, number = kernel(
        prepare_kernel,
        "prepare",
        [
            whole(fine_order), whole(state_deviation), whole(w_in), whole(trajectory), whole(biases),
            whole(sun_rank), whole(daylit_counts.reshape(1, DEVS)),
        ],
        [
            (all_groups, True),
            (shape((HID, COLS), f32), True),
            (shape((COLS, HID), bf16), True),
            (shape((1, COLS), f32), True),
        ],
        flops=2 * 10**9,
    )
    answer, token = kernel(
        answer_kernel,
        "answer",
        [whole(asked), whole(u), whole(number)],
        [(shape((SLOTS, HID), bf16), True), (shape((1, 128), f32), False)],
        scratch=[pltpu.VMEM((SLOTS, 128), f32)] * 2,
    )
    got = lax.all_to_all(answer.reshape(DEVS, CAP, HID), "cells", 0, 0, tiled=True)
    got = got.reshape(SLOTS, HID)
    links, border, part, first, second = kernel(
        build_kernel,
        "build",
        [
            whole(adjacent_source_slots), whole(outgoing_local_lists[0]), whole(forcing), state_rows,
            ("raw", token),
        ],
        [(all_links, "raw"), (all_border, True), (field, True), (side, True), (side, True)],
        scratch=[pltpu.VMEM((EXT, CELLS), bf16), pltpu.SemaphoreType.DMA((10,))],
        flops=3 * 10**9,
    )
    first, second = swap(first, second)

    groups, border, links, heat, temp, slope, part, heat_back, first, second = kernel(
        middle_kernel,
        "middle",
        [
            whole(got), whole(slot), whole(drive), whole(w_hidden), whole(w_out.T), whole(biases),
            whole(first), whole(second), whole(part), whole(forcing), state_rows,
            ("raw", groups), ("raw", border), ("raw", links),
        ],
        [
            (all_groups, False), (all_border, False), (all_links, False), (field, False),
            (field, False), (shape((3, HID, COLS), f32), False), (field, False), (field, False),
            (side, False), (side, False),
        ],
        scratch=[pltpu.SemaphoreType.DMA((7,))],
        limit=32,
        flops=5 * 10**9,
    )
    first, second = swap(first, second)
    (ahead,) = kernel(inner, "inner", [temp, heat, links], [(field, False)], limit=32)
    part, back, temp, first, second = kernel(
        third_kernel,
        "third",
        [first, second, border, part, heat_back, links, ahead],
        [
            (field, False), (shape((LEV, CELLS), bf16), False), (field, False), (side, False),
            (side, False),
        ],
        limit=32,
        flops=3 * 10**9,
    )
    first, second = swap(first, second)
    sens, top, ahead = kernel(
        window_kernel,
        "window",
        [temp, heat, links, slope, back, groups, whole(w_out.T), whole(w_hidden), whole(w_in)],
        [
            (shape((FEAT, CELLS), bf16), "raw"), (shape((TOP, CELLS), f32), False), (field, False),
        ],
        scratch=[pltpu.VMEM((FEAT - TOP, CELLS), bf16), pltpu.SemaphoreType.DMA],
        limit=32,
        flops=3 * 10**9,
    )
    sens, temp = kernel(
        finish_kernel,
        "finish",
        [first, second, border, part, links, ahead, top, ("raw", sens)],
        [(shape((FEAT, CELLS), bf16), "raw"), (field, True)],
        scratch=[pltpu.VMEM((TOP, CELLS), bf16), pltpu.SemaphoreType.DMA],
        limit=32,
        aliases={7: 0},
    )
    return temp, sens


def solution(mesh):
    return jax.shard_map(
        local,
        mesh=mesh,
        in_specs=(
            P(None, "cells"),
            P(None, "cells"),
            P(None, "cells"),
            P(),
            P(),
            P(),
            P(),
            P("cells", None),
            P("cells", None),
            P(),
            P("cells", None),
            P(None, "cells"),
            P("cells", None, None),
        ),
        out_specs=(P(None, "cells"), P(None, "cells")),
        check_vma=False,
    )
```

```python
import jax
import jax.numpy as jnp
from jax import lax
from jax.experimental import pallas as pl
from jax.experimental.pallas import tpu as pltpu
from jax.sharding import PartitionSpec as P

LEV, FEAT, HID = 90, 540, 256
COLS, CELLS, HALO = 512, 2048, 256
EXT = CELLS + 2 * HALO
DEVS, CAP = 128, 8
SLOTS = DEVS * CAP
KEEP, SPREAD = 0.25, 0.125
TOP = 96
PIECE = 512
OWN = CELLS // PIECE

f32, bf16, i32 = jnp.float32, jnp.bfloat16, jnp.int32
NN = (((1,), (0,)), ((), ()))
NT = (((1,), (1,)), ((), ()))
TN = (((0,), (0,)), ((), ()))


def dot(a, b, dims):
    return lax.dot_general(a, b, dims, preferred_element_type=f32)


def shape(dims, dtype):
    return jax.ShapeDtypeStruct(dims, dtype)


class Fetch:
    def __init__(self, source, ref, sems, rows, start):
        self.ref, self.rows, self.copies, self.done = ref, rows, [], set()
        for i in range(ref.shape[0] // rows):
            part = pl.ds(i * rows, rows)
            origin = source.at[pl.ds(start + i * rows, rows)]
            self.copies.append(pltpu.make_async_copy(origin, ref.at[part], sems.at[i]))

    def order(self):
        return [len(self.copies) - 1, *range(len(self.copies) - 1)]

    def __call__(self):
        for i in range(len(self.copies)):
            self.piece(i)
        return self.ref

    def piece(self, i):
        if i not in self.done:
            self.copies[i].wait()
            self.done.add(i)
        return self.ref.at[pl.ds(i * self.rows, self.rows)]


class Store:
    def __init__(self, target, ref, sem):
        self.ref = ref
        self.copy = pltpu.make_async_copy(ref, target, sem)

    def put(self):
        self.copy.start()


def kernel(body, name, args, outs, limit=48, flops=10**9, scratch=(), aliases=None):
    arrays, in_specs, plan, scratches = [], [], [], []
    for arg in args:
        if isinstance(arg, tuple) and arg[0] == "raw":
            arrays.append(pltpu.with_memory_space_constraint(arg[1], pltpu.HBM))
            in_specs.append(pl.BlockSpec(memory_space=pl.ANY))
            plan.append(None)
        elif isinstance(arg, tuple):
            array, rows, piece, *start = arg
            arrays.append(pltpu.with_memory_space_constraint(array, pltpu.HBM))
            in_specs.append(pl.BlockSpec(memory_space=pl.ANY))
            plan.append((piece, start[0] if start else 0))
            scratches.append(pltpu.VMEM((rows,) + array.shape[1:], array.dtype))
            scratches.append(pltpu.SemaphoreType.DMA((rows // piece,)))
        else:
            arrays.append(arg)
            in_specs.append(pl.BlockSpec(memory_space=pltpu.VMEM))
            plan.append(None)
    out_shapes, out_specs = [], []
    for out, far in outs:
        if far == "raw":
            out_shapes.append(pltpu.HBM(out.shape, out.dtype))
            out_specs.append(pl.BlockSpec(memory_space=pl.ANY))
        elif far:
            out_shapes.append(pltpu.HBM(out.shape, out.dtype))
            out_specs.append(pl.BlockSpec(memory_space=pl.ANY))
            scratches.append(pltpu.VMEM(out.shape, out.dtype))
            scratches.append(pltpu.SemaphoreType.DMA)
        else:
            out_shapes.append(out)
            out_specs.append(pl.BlockSpec(memory_space=pltpu.VMEM))

    def wrapped(*refs):
        ins, results = refs[: len(args)], refs[len(args) : len(args) + len(outs)]
        rest = list(refs[len(args) + len(outs) :])
        operands, targets = [], []
        for ref, how in zip(ins, plan):
            if how is None:
                operands.append(ref)
            else:
                place, sems = rest.pop(0), rest.pop(0)
                operands.append(Fetch(ref, place, sems, *how))
        for last in (False, True):
            for o in operands:
                if isinstance(o, Fetch) and (len(o.copies) > 1) == last:
                    for i in o.order():
                        o.copies[i].start()
        for ref, (out, far) in zip(results, outs):
            if far is True:
                targets.append(Store(ref, rest.pop(0), rest.pop(0)))
            else:
                targets.append(ref)
        body(*operands, *targets, *rest)
        for target in targets:
            if isinstance(target, Store):
                target.copy.wait()

    size = sum(a.size * a.dtype.itemsize for a in arrays)
    size += sum(o.size * o.dtype.itemsize for o, _ in outs)
    return pl.pallas_call(
        wrapped,
        out_shape=tuple(out_shapes),
        in_specs=in_specs,
        out_specs=tuple(out_specs),
        scratch_shapes=scratches + list(scratch),
        input_output_aliases=aliases or {},
        compiler_params=pltpu.CompilerParams(vmem_limit_bytes=limit * 1024 * 1024),
        cost_estimate=pl.CostEstimate(flops=flops, bytes_accessed=size, transcendentals=0),
        name=name,
    )(*arrays)


def whole(array):
    return (array, array.shape[0], array.shape[0])


def row_iota(rows, columns):
    return lax.broadcasted_iota(i32, (rows, columns), 0)


def lane_iota(rows, columns):
    return lax.broadcasted_iota(i32, (rows, columns), 1)


def onehot(mask):
    return jnp.where(mask, 1.0, 0.0).astype(bf16)


def pick_rows(index, block, columns):
    here = jnp.where(index >> 8 == block, index & 255, -1).astype(f32).astype(bf16)
    place = row_iota(256, columns).astype(f32).astype(bf16)
    return jnp.where(place == here, jnp.ones((), bf16), jnp.zeros((), bf16))


def to_column(row):
    return jnp.broadcast_to(row, (128, row.shape[1])).T[:, :1]


def chunk(i, size):
    return pl.ds(pl.multiple_of(i * size, size), size)


def route_kernel(parent_ref, request_ref, slot_ref):
    parents = parent_ref[...]
    target = parents >> 9
    column = (parents & (COLS - 1)) + 1
    target_column = to_column(target.astype(f32))
    same = (target_column == target.astype(f32)) & (row_iota(COLS, COLS) < lane_iota(COLS, COLS))
    rank = jnp.sum(jnp.where(same, 1.0, 0.0), axis=0, keepdims=True).astype(i32)
    slot_ref.ref[...] = target * CAP + rank
    slot_ref.put()
    owners = onehot(row_iota(DEVS, COLS) == target)
    ranked = row_iota(DEVS, COLS) == rank
    high = jnp.where(ranked, (column >> 4).astype(f32), 0.0).astype(bf16)
    low = jnp.where(ranked, (column & 15).astype(f32), 0.0).astype(bf16)
    request = dot(owners, high, NT) * 16.0 + dot(owners, low, NT)
    request_ref.ref[...] = request.reshape(DEVS, 1, 128)
    request_ref.put()


def prepare_kernel(
    order_ref, state_ref, w_in_ref, traj_ref, bias_ref, rank_ref, count_ref,
    groups_ref, drive_ref, u_ref, number_ref,
):
    me = lax.axis_index("cells")
    group = order_ref()[...] >> 2
    for c in range(8):
        sl = slice(c * 256, (c + 1) * 256)
        for b in range(2):
            groups_ref.ref[b * 256 : (b + 1) * 256, sl] = pick_rows(group[:, sl], b, 256)
    groups_ref.put()
    z = dot(traj_ref()[...], w_in_ref()[...], TN) + bias_ref()[0:1, :]
    decay = jnp.exp(-2.0 * jnp.minimum(jnp.abs(z), 30.0))
    u_ref.ref[...] = jnp.where(z < 0.0, -decay, decay).astype(bf16)
    u_ref.put()
    mine = jnp.where(lane_iota(1, DEVS) == me, count_ref()[...], 0).astype(f32)
    daylit = rank_ref()[...].astype(f32) < jnp.sum(mine, axis=1, keepdims=True)
    number_ref.ref[...] = jnp.where(daylit, lane_iota(1, COLS) + 1, -1).astype(f32)
    number_ref.put()
    mean = (0.25 * dot(state_ref()[...], groups_ref.ref[...], NT)).astype(bf16)
    drive_ref.ref[...] = dot(w_in_ref.ref[...], mean, TN)
    drive_ref.put()


def answer_kernel(request_ref, u_ref, number_ref, answer_ref, token_ref, left_ref, right_ref):
    request = request_ref[...].reshape(DEVS, 128)
    number = number_ref()[...]
    token_ref.ref[...] = number[:, :128]
    token_ref.put()
    chosen = [onehot(request[:, k : k + 1] == number) for k in range(CAP)]
    rows = dot(jnp.concatenate(chosen, axis=0), u_ref()[...], NN)
    for k in range(CAP):
        block = slice(k * DEVS, (k + 1) * DEVS)
        left_ref[pl.ds(k, DEVS, stride=CAP), :] = rows[block, :128]
        right_ref[pl.ds(k, DEVS, stride=CAP), :] = rows[block, 128:]
    answer_ref.ref[:, :128] = left_ref[...].astype(bf16)
    answer_ref.ref[:, 128:] = right_ref[...].astype(bf16)
    answer_ref.put()


def build_kernel(
    slots_ref, lists_ref, forcing_ref, state_ref, token_ref,
    links_ref, border_ref, part_ref, first_ref, second_ref, links, sems,
):
    even = (lax.axis_index("cells") & 1) == 0
    slots = slots_ref()[...]
    high = slots >> 8
    high = jnp.where(even & (high >= 8), 17 - high, high)
    low = slots & 255
    times = jnp.zeros((6, CELLS), f32)
    for k in range(6):
        times = times + jnp.where(slots == slots[k : k + 1, :], 1.0, 0.0)
    times = times.astype(bf16)
    lists = lists_ref()
    near = jnp.where(even, lists[1:2, :], lists[0:1, :])
    far = jnp.where(even, lists[0:1, :], lists[1:2, :])
    forcing = forcing_ref()

    def fill(jb):
        here = jnp.where(high == jb, low, -1).astype(f32).astype(bf16)
        for c in range(8):
            sl = slice(c * 256, (c + 1) * 256)
            place = row_iota(256, 256).astype(f32).astype(bf16)
            count = jnp.zeros((256, 256), bf16)
            for k in range(6):
                count = jnp.where(here[k : k + 1, sl] == place, times[k : k + 1, sl], count)
            links[jb * 256 : (jb + 1) * 256, sl] = count

    def share(jb):
        return SPREAD * dot(forcing[...], links[jb * 256 : (jb + 1) * 256, :], NT)

    def out(jb):
        rows = pl.ds(jb * 256, 256)
        return pltpu.make_async_copy(links.at[rows], links_ref.at[rows], sems.at[jb])

    def consume(jb):
        if jb == 8:
            first_ref.ref[0] = share(jb).astype(bf16)
        elif jb == 9:
            second_ref.ref[0] = share(jb).astype(bf16)
        else:
            sl = slice(jb * 256, (jb + 1) * 256)
            part_ref.ref[:, sl] = KEEP * forcing[:, sl].astype(f32) + share(jb)

    for b in range(8):
        sl = slice(b * 256, (b + 1) * 256)
        border_ref.ref[sl, :HALO] = pick_rows(near, b, 256)
        border_ref.ref[sl, HALO:] = pick_rows(far, b, 256)
    border_ref.put()
    state = state_ref()
    border = dot(state[:LEV, :], border_ref.ref[...], NN)
    first_ref.ref[1] = border[:, :HALO].astype(bf16)
    second_ref.ref[1] = border[:, HALO:].astype(bf16)
    order = (8, 9, *range(8))
    fill(order[0])
    for now, later in zip(order, order[1:] + (None,)):
        if later is not None:
            fill(later)
        consume(now)
        out(now).start()
    first_ref.put()
    second_ref.put()
    part_ref.put()
    for jb in range(10):
        out(jb).wait()


def received(first, second, border):
    return dot(first, border[:, :HALO], NT) + dot(second, border[:, HALO:], NT)


def push(rounded, links, first_ref, second_ref):
    share = SPREAD * dot(rounded, links[CELLS:, :], NT)
    first_ref[0] = share[:, :HALO].astype(bf16)
    second_ref[0] = share[:, HALO:].astype(bf16)


def pull(adjoint_ref, links, part_ref):
    rounded = adjoint_ref[...].astype(bf16)
    for i in range(OWN):
        sl = slice(i * PIECE, (i + 1) * PIECE)
        part_ref[:, sl] = KEEP * adjoint_ref[:, sl] + SPREAD * dot(rounded, links[sl, :], NT)


def send_border(temp, border, first_ref, second_ref):
    values = dot(temp.astype(bf16), border[...], NN)
    first_ref[1] = values[:, :HALO].astype(bf16)
    second_ref[1] = values[:, HALO:].astype(bf16)


def network_kernel(
    answer_ref, slot_ref, drive_ref, w_hidden_ref, w_out_ref, bias_ref, state_ref,
    groups_far, border_far, links_far,
    groups, border, links, heat_ref, slope_ref, ahead_ref,
    sems,
):
    groups_copy = pltpu.make_async_copy(groups_far, groups, sems.at[5])
    border_copy = pltpu.make_async_copy(border_far, border, sems.at[6])

    def piece(i):
        rows = pl.ds(i * PIECE, PIECE)
        return pltpu.make_async_copy(links_far.at[rows], links.at[rows], sems.at[i])

    groups_copy.start()
    for i in range(OWN + 1):
        piece(i).start()
    border_copy.start()

    slots = slot_ref()[...]
    chosen = jnp.concatenate([pick_rows(slots, b, COLS) for b in range(SLOTS // 256)], axis=0)
    u = dot(answer_ref()[...], chosen, TN)
    size = jnp.abs(u)
    inverse = 1.0 / (1.0 + size)
    act = jnp.where(u < 0.0, size - 1.0, 1.0 - size) * inverse
    slope = 4.0 * size * inverse * inverse
    slope_ref[0] = slope
    tangent = (slope * drive_ref()[...]).astype(bf16)
    weights, biases = w_hidden_ref(), bias_ref()
    for layer in range(2):
        weight = weights[layer]
        bias = to_column(biases[layer + 1 : layer + 2, :])
        act = jnp.tanh(dot(weight, act.astype(bf16), TN) + bias)
        slope = 1.0 - act * act
        slope_ref[layer + 1] = slope
        tangent = (slope * dot(weight, tangent, TN)).astype(bf16)
    heating = dot(w_out_ref()[...], tangent, NN).astype(bf16)
    groups_copy.wait()
    heat_ref[...] = dot(heating, groups[...], NN)
    for i in range(OWN):
        piece(i).wait()
    inner(state_ref(), heat_ref, links, ahead_ref)
    piece(OWN).wait()
    border_copy.wait()


def second_kernel(
    first_in, second_in, border, part_in, forcing_ref, links, ahead_ref,
    adjoint_ref, heat_back_ref, temp_ref, first_ref, second_ref,
):
    adjoint = part_in()[...] + received(first_in[0], second_in[0], border)
    adjoint_ref[...] = adjoint
    push(adjoint.astype(bf16), links, first_ref, second_ref)
    temp = outer(ahead_ref, first_in[1], second_in[1], links)
    temp_ref[...] = temp
    send_border(temp, border, first_ref, second_ref)
    heat_back_ref[...] = forcing_ref()[...].astype(f32) + adjoint


def inner(temp_ref, heat_ref, links, part_ref):
    rounded = temp_ref[:LEV, :].astype(bf16)
    for i in range(OWN):
        sl = slice(i * PIECE, (i + 1) * PIECE)
        part_ref[:, sl] = (
            KEEP * temp_ref[:LEV, sl].astype(f32)
            + heat_ref[:, sl]
            + SPREAD * dot(rounded, links[:CELLS, sl], NN)
        )


def outer(part_ref, first, second, links):
    sides = jnp.concatenate([first, second], axis=1)
    return part_ref[...] + SPREAD * dot(sides, links[CELLS:, :], NN)


def between_kernel(adjoint_ref, temp_ref, heat_ref, links, part_ref, ahead_ref):
    pull(adjoint_ref, links, part_ref)
    inner(temp_ref, heat_ref, links, ahead_ref)


def third_kernel(
    first_in, second_in, border, part_in, heat_back_ref, links, ahead_ref,
    adjoint_ref, back_ref, temp_ref, first_ref, second_ref,
):
    adjoint = part_in[...] + received(first_in[0], second_in[0], border)
    adjoint_ref[...] = adjoint
    push(adjoint.astype(bf16), links, first_ref, second_ref)
    temp = outer(ahead_ref, first_in[1], second_in[1], links)
    temp_ref[...] = temp
    send_border(temp, border, first_ref, second_ref)
    back_ref[...] = (heat_back_ref[...] + adjoint).astype(bf16)


def window_kernel(
    adjoint_ref, temp_ref, heat_ref, links, slope_ref, back_ref, groups, w_out_ref, w_hidden_ref,
    w_in_ref, sens_far, top_ref, part_ref, ahead_ref, low_ref, sem,
):
    inputs = dot(back_ref[...], groups[...], NT).astype(bf16)
    weights = w_hidden_ref()
    back = (slope_ref[2] * dot(w_out_ref()[...], inputs, TN)).astype(bf16)
    back = (slope_ref[1] * dot(weights[1], back, NN)).astype(bf16)
    back = (slope_ref[0] * dot(weights[0], back, NN)).astype(bf16)
    sens = (0.25 * dot(w_in_ref()[...], back, NN)).astype(bf16)
    low_ref[...] = dot(sens[TOP:], groups[...], NN).astype(bf16)
    copy = pltpu.make_async_copy(low_ref, sens_far.at[pl.ds(TOP, FEAT - TOP)], sem)
    copy.start()
    top_ref[...] = dot(sens[:TOP], groups[...], NN)
    inner(temp_ref, heat_ref, links, ahead_ref)
    pull(adjoint_ref, links, part_ref)
    copy.wait()


def finish_kernel(
    first_in, second_in, border, part_in, links, ahead_ref, top_in, sens_in,
    sens_far, temp_far, top_ref, sem,
):
    temp_far.ref[...] = outer(ahead_ref, first_in[1], second_in[1], links)
    temp_far.put()
    adjoint = part_in[...] + received(first_in[0], second_in[0], border)
    top_ref[:LEV] = (top_in[:LEV] + adjoint).astype(bf16)
    top_ref[LEV:] = top_in[LEV:].astype(bf16)
    copy = pltpu.make_async_copy(top_ref, sens_far.at[pl.ds(0, TOP)], sem)
    copy.start()
    copy.wait()


def local(
    state_deviation, forcing, trajectory, w_in, w_hidden, w_out, biases, fine_order, group_parent,
    daylit_counts, sun_rank, adjacent_source_slots, outgoing_local_lists,
):
    near_pairs = [(i, i ^ 1) for i in range(DEVS)]
    far_pairs = [(i, (i + 1) % DEVS if i % 2 else (i - 1) % DEVS) for i in range(DEVS)]

    def swap(first, second):
        second = lax.ppermute(second, "cells", far_pairs)
        return lax.ppermute(first, "cells", near_pairs), second

    request, slot = kernel(
        route_kernel,
        "route",
        [group_parent],
        [(shape((DEVS, 1, 128), f32), True), (shape((1, COLS), i32), True)],
        flops=10**7,
    )
    asked = lax.all_to_all(request, "cells", 0, 0, tiled=True)

    side = shape((2, LEV, HALO), bf16)
    field = shape((LEV, CELLS), f32)
    all_links, all_border = shape((EXT, CELLS), bf16), shape((CELLS, 2 * HALO), bf16)
    all_groups = shape((COLS, CELLS), bf16)
    state_rows = (state_deviation, TOP, TOP)

    groups, drive, u, number = kernel(
        prepare_kernel,
        "prepare",
        [
            whole(fine_order), whole(state_deviation), whole(w_in), whole(trajectory), whole(biases),
            whole(sun_rank), whole(daylit_counts.reshape(1, DEVS)),
        ],
        [
            (all_groups, True),
            (shape((HID, COLS), f32), True),
            (shape((COLS, HID), bf16), True),
            (shape((1, COLS), f32), True),
        ],
        flops=2 * 10**9,
    )
    answer, token = kernel(
        answer_kernel,
        "answer",
        [asked, whole(u), whole(number)],
        [(shape((SLOTS, HID), bf16), True), (shape((1, 128), f32), True)],
        scratch=[pltpu.VMEM((SLOTS, 128), f32)] * 2,
    )
    got = lax.all_to_all(answer.reshape(DEVS, CAP, HID), "cells", 0, 0, tiled=True)
    got = got.reshape(SLOTS, HID)
    links, border, part, first, second = kernel(
        build_kernel,
        "build",
        [
            whole(adjacent_source_slots), whole(outgoing_local_lists[0]), whole(forcing), state_rows,
            ("raw", token),
        ],
        [(all_links, "raw"), (all_border, True), (field, True), (side, True), (side, True)],
        scratch=[pltpu.VMEM((EXT, CELLS), bf16), pltpu.SemaphoreType.DMA((10,))],
        flops=3 * 10**9,
    )
    first, second = swap(first, second)

    near = (field, False)
    groups, border, links, heat, slope, ahead = kernel(
        network_kernel,
        "network",
        [
            whole(got), whole(slot), whole(drive), whole(w_hidden), whole(w_out.T), whole(biases),
            state_rows, ("raw", groups), ("raw", border), ("raw", links),
        ],
        [
            (all_groups, False), (all_border, False), (all_links, False), near,
            (shape((3, HID, COLS), f32), False), near,
        ],
        scratch=[pltpu.SemaphoreType.DMA((7,))],
        limit=32,
        flops=5 * 10**9,
    )
    adjoint, heat_back, temp, first, second = kernel(
        second_kernel,
        "second",
        [first, second, border, whole(part), whole(forcing), links, ahead],
        [near, near, near, (side, False), (side, False)],
        limit=32,
    )
    first, second = swap(first, second)
    part, ahead = kernel(
        between_kernel, "between", [adjoint, temp, heat, links], [near, near], limit=32
    )
    adjoint, back, temp, first, second = kernel(
        third_kernel,
        "third",
        [first, second, border, part, heat_back, links, ahead],
        [near, (shape((LEV, CELLS), bf16), False), near, (side, False), (side, False)],
        limit=32,
    )
    first, second = swap(first, second)
    sens, top, part, ahead = kernel(
        window_kernel,
        "window",
        [
            adjoint, temp, heat, links, slope, back, groups, whole(w_out.T), whole(w_hidden),
            whole(w_in),
        ],
        [
            (shape((FEAT, CELLS), bf16), "raw"), (shape((TOP, CELLS), f32), False), near, near,
        ],
        scratch=[pltpu.VMEM((FEAT - TOP, CELLS), bf16), pltpu.SemaphoreType.DMA],
        limit=32,
        flops=3 * 10**9,
    )
    sens, temp = kernel(
        finish_kernel,
        "finish",
        [first, second, border, part, links, ahead, top, ("raw", sens)],
        [(shape((FEAT, CELLS), bf16), "raw"), (field, True)],
        scratch=[pltpu.VMEM((TOP, CELLS), bf16), pltpu.SemaphoreType.DMA],
        limit=32,
        aliases={7: 0},
    )
    return temp, sens


def solution(mesh):
    return jax.shard_map(
        local,
        mesh=mesh,
        in_specs=(
            P(None, "cells"),
            P(None, "cells"),
            P(None, "cells"),
            P(),
            P(),
            P(),
            P(),
            P("cells", None),
            P("cells", None),
            P(),
            P("cells", None),
            P(None, "cells"),
            P("cells", None, None),
        ),
        out_specs=(P(None, "cells"), P(None, "cells")),
        check_vma=False,
    )
```

```python
import jax
import jax.numpy as jnp
from jax import lax
from jax.experimental import pallas as pl
from jax.experimental.pallas import tpu as pltpu
from jax.sharding import PartitionSpec as P

LEV, FEAT, HID = 90, 540, 256
COLS, CELLS, HALO = 512, 2048, 256
EXT = CELLS + 2 * HALO
DEVS, CAP = 128, 8
SLOTS = DEVS * CAP
KEEP, SPREAD = 0.25, 0.125
TOP = 96
PIECE = 512
OWN = CELLS // PIECE

f32, bf16, i32 = jnp.float32, jnp.bfloat16, jnp.int32
NN = (((1,), (0,)), ((), ()))
NT = (((1,), (1,)), ((), ()))
TN = (((0,), (0,)), ((), ()))


def dot(a, b, dims):
    return lax.dot_general(a, b, dims, preferred_element_type=f32)


def shape(dims, dtype):
    return jax.ShapeDtypeStruct(dims, dtype)


class Fetch:
    def __init__(self, source, ref, sems, rows, start):
        self.ref, self.rows, self.copies, self.done = ref, rows, [], set()
        for i in range(ref.shape[0] // rows):
            part = pl.ds(i * rows, rows)
            origin = source.at[pl.ds(start + i * rows, rows)]
            self.copies.append(pltpu.make_async_copy(origin, ref.at[part], sems.at[i]))

    def order(self):
        return [len(self.copies) - 1, *range(len(self.copies) - 1)]

    def __call__(self):
        for i in range(len(self.copies)):
            self.piece(i)
        return self.ref

    def piece(self, i):
        if i not in self.done:
            self.copies[i].wait()
            self.done.add(i)
        return self.ref.at[pl.ds(i * self.rows, self.rows)]


class Store:
    def __init__(self, target, ref, sem):
        self.ref = ref
        self.copy = pltpu.make_async_copy(ref, target, sem)

    def put(self):
        self.copy.start()


def kernel(body, name, args, outs, limit=48, flops=10**9, scratch=(), aliases=None):
    arrays, in_specs, plan, scratches = [], [], [], []
    for arg in args:
        if isinstance(arg, tuple) and arg[0] == "raw":
            arrays.append(pltpu.with_memory_space_constraint(arg[1], pltpu.HBM))
            in_specs.append(pl.BlockSpec(memory_space=pl.ANY))
            plan.append(None)
        elif isinstance(arg, tuple):
            array, rows, piece, *start = arg
            arrays.append(pltpu.with_memory_space_constraint(array, pltpu.HBM))
            in_specs.append(pl.BlockSpec(memory_space=pl.ANY))
            plan.append((piece, start[0] if start else 0))
            scratches.append(pltpu.VMEM((rows,) + array.shape[1:], array.dtype))
            scratches.append(pltpu.SemaphoreType.DMA((rows // piece,)))
        else:
            arrays.append(arg)
            in_specs.append(pl.BlockSpec(memory_space=pltpu.VMEM))
            plan.append(None)
    out_shapes, out_specs = [], []
    for out, far in outs:
        if far == "raw":
            out_shapes.append(pltpu.HBM(out.shape, out.dtype))
            out_specs.append(pl.BlockSpec(memory_space=pl.ANY))
        elif far:
            out_shapes.append(pltpu.HBM(out.shape, out.dtype))
            out_specs.append(pl.BlockSpec(memory_space=pl.ANY))
            scratches.append(pltpu.VMEM(out.shape, out.dtype))
            scratches.append(pltpu.SemaphoreType.DMA)
        else:
            out_shapes.append(out)
            out_specs.append(pl.BlockSpec(memory_space=pltpu.VMEM))

    def wrapped(*refs):
        ins, results = refs[: len(args)], refs[len(args) : len(args) + len(outs)]
        rest = list(refs[len(args) + len(outs) :])
        operands, targets = [], []
        for ref, how in zip(ins, plan):
            if how is None:
                operands.append(ref)
            else:
                place, sems = rest.pop(0), rest.pop(0)
                operands.append(Fetch(ref, place, sems, *how))
        for last in (False, True):
            for o in operands:
                if isinstance(o, Fetch) and (len(o.copies) > 1) == last:
                    for i in o.order():
                        o.copies[i].start()
        for ref, (out, far) in zip(results, outs):
            if far is True:
                targets.append(Store(ref, rest.pop(0), rest.pop(0)))
            else:
                targets.append(ref)
        body(*operands, *targets, *rest)
        for target in targets:
            if isinstance(target, Store):
                target.copy.wait()

    size = sum(a.size * a.dtype.itemsize for a in arrays)
    size += sum(o.size * o.dtype.itemsize for o, _ in outs)
    return pl.pallas_call(
        wrapped,
        out_shape=tuple(out_shapes),
        in_specs=in_specs,
        out_specs=tuple(out_specs),
        scratch_shapes=scratches + list(scratch),
        input_output_aliases=aliases or {},
        compiler_params=pltpu.CompilerParams(vmem_limit_bytes=limit * 1024 * 1024),
        cost_estimate=pl.CostEstimate(flops=flops, bytes_accessed=size, transcendentals=0),
        name=name,
    )(*arrays)


def whole(array):
    return (array, array.shape[0], array.shape[0])


def row_iota(rows, columns):
    return lax.broadcasted_iota(i32, (rows, columns), 0)


def lane_iota(rows, columns):
    return lax.broadcasted_iota(i32, (rows, columns), 1)


def onehot(mask):
    return jnp.where(mask, 1.0, 0.0).astype(bf16)


def pick_rows(index, block, columns):
    here = jnp.where(index >> 8 == block, index & 255, -1).astype(f32).astype(bf16)
    place = row_iota(256, columns).astype(f32).astype(bf16)
    return jnp.where(place == here, jnp.ones((), bf16), jnp.zeros((), bf16))


def make_groups(order_ref, groups_ref):
    group = order_ref[...] >> 2
    for c in range(8):
        sl = slice(c * 256, (c + 1) * 256)
        for b in range(2):
            groups_ref[b * 256 : (b + 1) * 256, sl] = pick_rows(group[:, sl], b, 256)


def make_border(lists_ref, border_ref):
    even = (lax.axis_index("cells") & 1) == 0
    near = jnp.where(even, lists_ref[1:2, :], lists_ref[0:1, :])
    far = jnp.where(even, lists_ref[0:1, :], lists_ref[1:2, :])
    for b in range(8):
        sl = slice(b * 256, (b + 1) * 256)
        border_ref[sl, :HALO] = pick_rows(near, b, 256)
        border_ref[sl, HALO:] = pick_rows(far, b, 256)


def to_column(row):
    return jnp.broadcast_to(row, (128, row.shape[1])).T[:, :1]


def chunk(i, size):
    return pl.ds(pl.multiple_of(i * size, size), size)


def route_kernel(parent_ref, request_ref, slot_ref):
    parents = parent_ref[...]
    target = parents >> 9
    column = (parents & (COLS - 1)) + 1
    target_column = to_column(target.astype(f32))
    same = (target_column == target.astype(f32)) & (row_iota(COLS, COLS) < lane_iota(COLS, COLS))
    rank = jnp.sum(jnp.where(same, 1.0, 0.0), axis=0, keepdims=True).astype(i32)
    slot_ref.ref[...] = target * CAP + rank
    slot_ref.put()
    owners = onehot(row_iota(DEVS, COLS) == target)
    ranked = row_iota(DEVS, COLS) == rank
    high = jnp.where(ranked, (column >> 4).astype(f32), 0.0).astype(bf16)
    low = jnp.where(ranked, (column & 15).astype(f32), 0.0).astype(bf16)
    request = dot(owners, high, NT) * 16.0 + dot(owners, low, NT)
    request_ref.ref[...] = request.reshape(DEVS, 1, 128)
    request_ref.put()


def prepare_kernel(
    order_ref, state_ref, w_in_ref, traj_ref, bias_ref, rank_ref, count_ref, drive_ref, u_ref, groups
):
    me = lax.axis_index("cells")
    z = dot(traj_ref()[...], w_in_ref()[...], TN) + bias_ref()[0:1, :]
    decay = jnp.exp(-2.0 * jnp.minimum(jnp.abs(z), 30.0))
    mine = jnp.where(lane_iota(1, DEVS) == me, count_ref()[...], 0).astype(f32)
    daylit = rank_ref()[...].astype(f32) < jnp.sum(mine, axis=1, keepdims=True)
    daylit = to_column(jnp.where(daylit, 1.0, 0.0)) > 0.5
    u = jnp.where(z < 0.0, -decay, decay)
    u_ref.ref[...] = jnp.where(daylit, u, 0.0).astype(bf16)
    u_ref.put()
    make_groups(order_ref(), groups)
    mean = (0.25 * dot(state_ref()[...], groups[...], NT)).astype(bf16)
    drive_ref.ref[...] = dot(w_in_ref.ref[...], mean, TN)
    drive_ref.put()


def answer_kernel(
    request_ref, u_ref, answer_ref, token_ref, left_ref, right_ref, whole_ref, sems
):
    request = request_ref[...].reshape(DEVS, 128)
    token_ref.ref[...] = request[:1, :]
    token_ref.put()
    number = (lane_iota(1, COLS) + 1).astype(f32)
    half = DEVS // 2
    chosen = [
        jnp.concatenate(
            [onehot(request[h * half : (h + 1) * half, k : k + 1] == number) for k in range(CAP)],
            axis=0,
        )
        for h in range(2)
    ]
    u = u_ref()[...]
    copies = []
    for h in range(2):
        rows = dot(chosen[h], u, NN)
        for k in range(CAP):
            block = slice(k * half, (k + 1) * half)
            place = pl.ds(h * half * CAP + k, half, stride=CAP)
            left_ref[place, :] = rows[block, :128]
            right_ref[place, :] = rows[block, 128:]
        part = slice(h * half * CAP, (h + 1) * half * CAP)
        whole_ref[part, :128] = left_ref[part, :].astype(bf16)
        whole_ref[part, 128:] = right_ref[part, :].astype(bf16)
        window = pl.ds(h * half * CAP, half * CAP)
        copy = pltpu.make_async_copy(whole_ref.at[window], answer_ref.at[window], sems.at[h])
        copy.start()
        copies.append(copy)
    for copy in copies:
        copy.wait()


def build_kernel(
    slots_ref, lists_ref, forcing_ref, state_ref, token_ref,
    links_ref, part_ref, first_ref, second_ref, links, border_ref, sems,
):
    even = (lax.axis_index("cells") & 1) == 0
    slots = slots_ref()[...]
    high = slots >> 8
    high = jnp.where(even & (high >= 8), 17 - high, high)
    low = slots & 255
    times = jnp.zeros((6, CELLS), f32)
    for k in range(6):
        times = times + jnp.where(slots == slots[k : k + 1, :], 1.0, 0.0)
    times = times.astype(bf16)
    forcing = forcing_ref()

    def fill(jb):
        here = jnp.where(high == jb, low, -1).astype(f32).astype(bf16)
        for c in range(8):
            sl = slice(c * 256, (c + 1) * 256)
            place = row_iota(256, 256).astype(f32).astype(bf16)
            count = jnp.zeros((256, 256), bf16)
            for k in range(6):
                count = jnp.where(here[k : k + 1, sl] == place, times[k : k + 1, sl], count)
            links[jb * 256 : (jb + 1) * 256, sl] = count

    def share(jb):
        return SPREAD * dot(forcing[...], links[jb * 256 : (jb + 1) * 256, :], NT)

    def out(jb):
        rows = pl.ds(jb * 256, 256)
        return pltpu.make_async_copy(links.at[rows], links_ref.at[rows], sems.at[jb])

    def consume(jb):
        if jb == 8:
            first_ref.ref[0] = share(jb).astype(bf16)
        elif jb == 9:
            second_ref.ref[0] = share(jb).astype(bf16)
        else:
            sl = slice(jb * 256, (jb + 1) * 256)
            part_ref.ref[:, sl] = KEEP * forcing[:, sl].astype(f32) + share(jb)

    make_border(lists_ref(), border_ref)
    state = state_ref()
    border = dot(state[:LEV, :], border_ref[...], NN)
    first_ref.ref[1] = border[:, :HALO].astype(bf16)
    second_ref.ref[1] = border[:, HALO:].astype(bf16)
    order = (8, 9, *range(8))
    fill(order[0])
    for now, later in zip(order, order[1:] + (None,)):
        if later is not None:
            fill(later)
        consume(now)
        out(now).start()
    first_ref.put()
    second_ref.put()
    part_ref.put()
    for jb in range(10):
        out(jb).wait()


def received(first, second, border):
    return dot(first, border[:, :HALO], NT) + dot(second, border[:, HALO:], NT)


def push(rounded, links, first_ref, second_ref):
    share = SPREAD * dot(rounded, links[CELLS:, :], NT)
    first_ref[0] = share[:, :HALO].astype(bf16)
    second_ref[0] = share[:, HALO:].astype(bf16)


def pull(adjoint_ref, links, part_ref):
    rounded = adjoint_ref[...].astype(bf16)
    for i in range(OWN):
        sl = slice(i * PIECE, (i + 1) * PIECE)
        part_ref[:, sl] = KEEP * adjoint_ref[:, sl] + SPREAD * dot(rounded, links[sl, :], NT)


def send_border(temp, border, first_ref, second_ref):
    values = dot(temp.astype(bf16), border[...], NN)
    first_ref[1] = values[:, :HALO].astype(bf16)
    second_ref[1] = values[:, HALO:].astype(bf16)


def network_kernel(
    answer_ref, slot_ref, drive_ref, w_hidden_ref, w_out_ref, bias_ref, order_ref, lists_ref,
    state_ref, links_far, part_far, forcing_far,
    groups, border, links, heat_ref, slope_ref, ahead_ref, part_ref, forcing_ref,
    sems,
):
    def piece(i):
        rows = pl.ds(i * PIECE, PIECE)
        return pltpu.make_async_copy(links_far.at[rows], links.at[rows], sems.at[i])

    later = [
        pltpu.make_async_copy(part_far, part_ref, sems.at[OWN + 1]),
        pltpu.make_async_copy(forcing_far, forcing_ref, sems.at[OWN + 2]),
    ]
    for i in range(OWN + 1):
        piece(i).start()
    for copy in later:
        copy.start()

    make_groups(order_ref(), groups)
    make_border(lists_ref(), border)
    slots = slot_ref()[...]
    chosen = jnp.concatenate([pick_rows(slots, b, COLS) for b in range(SLOTS // 256)], axis=0)
    u = dot(answer_ref[...], chosen, TN)
    size = jnp.abs(u)
    inverse = 1.0 / (1.0 + size)
    act = jnp.where(u < 0.0, size - 1.0, 1.0 - size) * inverse
    slope = 4.0 * size * inverse * inverse
    slope_ref[0] = slope
    tangent = (slope * drive_ref()[...]).astype(bf16)
    weights, biases = w_hidden_ref(), bias_ref()
    for layer in range(2):
        weight = weights[layer]
        bias = to_column(biases[layer + 1 : layer + 2, :])
        act = jnp.tanh(dot(weight, act.astype(bf16), TN) + bias)
        slope = 1.0 - act * act
        slope_ref[layer + 1] = slope
        tangent = (slope * dot(weight, tangent, TN)).astype(bf16)
    heating = dot(w_out_ref()[...], tangent, NN).astype(bf16)
    heat_ref[...] = dot(heating, groups[...], NN)
    state = state_ref()
    ahead_ref[...] = KEEP * state[:LEV, :].astype(f32) + heat_ref[...]
    for i in range(OWN):
        piece(i).wait()
        sl = slice(i * PIECE, (i + 1) * PIECE)
        ahead_ref[...] += SPREAD * dot(state[:LEV, sl], links[sl, :], NN)
    piece(OWN).wait()
    for copy in later:
        copy.wait()


def second_kernel(
    first_in, second_in, border, part_in, forcing_ref, links, ahead_ref,
    adjoint_ref, heat_back_ref, temp_ref, first_ref, second_ref,
):
    adjoint = part_in[...] + received(first_in[0], second_in[0], border)
    adjoint_ref[...] = adjoint
    push(adjoint.astype(bf16), links, first_ref, second_ref)
    temp = outer(ahead_ref, first_in[1], second_in[1], links)
    temp_ref[...] = temp
    send_border(temp, border, first_ref, second_ref)
    heat_back_ref[...] = forcing_ref[...].astype(f32) + adjoint


def inner(temp_ref, heat_ref, links, part_ref):
    rounded = temp_ref[:LEV, :].astype(bf16)
    for i in range(OWN):
        sl = slice(i * PIECE, (i + 1) * PIECE)
        part_ref[:, sl] = (
            KEEP * temp_ref[:LEV, sl].astype(f32)
            + heat_ref[:, sl]
            + SPREAD * dot(rounded, links[:CELLS, sl], NN)
        )


def outer(part_ref, first, second, links):
    sides = jnp.concatenate([first, second], axis=1)
    return part_ref[...] + SPREAD * dot(sides, links[CELLS:, :], NN)


def between_kernel(adjoint_ref, temp_ref, heat_ref, links, part_ref, ahead_ref):
    pull(adjoint_ref, links, part_ref)
    inner(temp_ref, heat_ref, links, ahead_ref)


def third_kernel(
    first_in, second_in, border, part_in, heat_back_ref, links, ahead_ref,
    adjoint_ref, back_ref, temp_ref, first_ref, second_ref,
):
    adjoint = part_in[...] + received(first_in[0], second_in[0], border)
    adjoint_ref[...] = adjoint
    push(adjoint.astype(bf16), links, first_ref, second_ref)
    temp = outer(ahead_ref, first_in[1], second_in[1], links)
    temp_ref[...] = temp
    send_border(temp, border, first_ref, second_ref)
    back_ref[...] = (heat_back_ref[...] + adjoint).astype(bf16)


def window_kernel(
    adjoint_ref, temp_ref, heat_ref, links, slope_ref, back_ref, groups, w_out_ref, w_hidden_ref,
    w_in_ref, sens_far, top_ref, part_ref, ahead_ref, low_ref, sem,
):
    inner(temp_ref, heat_ref, links, ahead_ref)
    inputs = dot(back_ref[...], groups[...], NT).astype(bf16)
    weights = w_hidden_ref()
    back = (slope_ref[2] * dot(w_out_ref()[...], inputs, TN)).astype(bf16)
    back = (slope_ref[1] * dot(weights[1], back, NN)).astype(bf16)
    back = (slope_ref[0] * dot(weights[0], back, NN)).astype(bf16)
    sens = (0.25 * dot(w_in_ref()[...], back, NN)).astype(bf16)
    low_ref[...] = dot(sens[TOP:], groups[...], NN).astype(bf16)
    copy = pltpu.make_async_copy(low_ref, sens_far.at[pl.ds(TOP, FEAT - TOP)], sem)
    copy.start()
    top_ref[...] = dot(sens[:TOP], groups[...], NN)
    pull(adjoint_ref, links, part_ref)
    copy.wait()


def finish_kernel(
    first_in, second_in, border, part_in, links, ahead_ref, top_in, sens_in,
    sens_far, temp_far, top_ref, sem,
):
    temp_far.ref[...] = outer(ahead_ref, first_in[1], second_in[1], links)
    temp_far.put()
    adjoint = part_in[...] + received(first_in[0], second_in[0], border)
    top_ref[:LEV] = (top_in[:LEV] + adjoint).astype(bf16)
    top_ref[LEV:] = top_in[LEV:].astype(bf16)
    copy = pltpu.make_async_copy(top_ref, sens_far.at[pl.ds(0, TOP)], sem)
    copy.start()
    copy.wait()


def local(
    state_deviation, forcing, trajectory, w_in, w_hidden, w_out, biases, fine_order, group_parent,
    daylit_counts, sun_rank, adjacent_source_slots, outgoing_local_lists,
):
    near_pairs = [(i, i ^ 1) for i in range(DEVS)]
    far_pairs = [(i, (i + 1) % DEVS if i % 2 else (i - 1) % DEVS) for i in range(DEVS)]

    def swap(first, second):
        second = lax.ppermute(second, "cells", far_pairs)
        return lax.ppermute(first, "cells", near_pairs), second

    request, slot = kernel(
        route_kernel,
        "route",
        [group_parent],
        [(shape((DEVS, 1, 128), f32), True), (shape((1, COLS), i32), True)],
        flops=10**7,
    )
    asked = lax.all_to_all(request, "cells", 0, 0, tiled=True)

    side = shape((2, LEV, HALO), bf16)
    field = shape((LEV, CELLS), f32)
    all_links, all_border = shape((EXT, CELLS), bf16), shape((CELLS, 2 * HALO), bf16)
    all_groups = shape((COLS, CELLS), bf16)
    state_rows = (state_deviation, TOP, TOP)

    drive, u = kernel(
        prepare_kernel,
        "prepare",
        [
            whole(fine_order), whole(state_deviation), whole(w_in), whole(trajectory), whole(biases),
            whole(sun_rank), whole(daylit_counts.reshape(1, DEVS)),
        ],
        [(shape((HID, COLS), f32), True), (shape((COLS, HID), bf16), True)],
        scratch=[pltpu.VMEM((COLS, CELLS), bf16)],
        flops=2 * 10**9,
    )
    answer, token = kernel(
        answer_kernel,
        "answer",
        [asked, whole(u)],
        [(shape((SLOTS, HID), bf16), "raw"), (shape((1, 128), f32), True)],
        scratch=[
            pltpu.VMEM((SLOTS, 128), f32),
            pltpu.VMEM((SLOTS, 128), f32),
            pltpu.VMEM((SLOTS, HID), bf16),
            pltpu.SemaphoreType.DMA((2,)),
        ],
    )
    got = lax.all_to_all(answer.reshape(DEVS, CAP, HID), "cells", 0, 0, tiled=True)
    got = got.reshape(SLOTS, HID)
    links, part, first, second = kernel(
        build_kernel,
        "build",
        [
            whole(adjacent_source_slots), whole(outgoing_local_lists[0]), whole(forcing), state_rows,
            ("raw", token),
        ],
        [(all_links, "raw"), (field, True), (side, True), (side, True)],
        scratch=[
            pltpu.VMEM((EXT, CELLS), bf16),
            pltpu.VMEM((CELLS, 2 * HALO), bf16),
            pltpu.SemaphoreType.DMA((10,)),
        ],
        flops=3 * 10**9,
    )
    first, second = swap(first, second)

    near = (field, False)
    groups, border, links, heat, slope, ahead, part, late_forcing = kernel(
        network_kernel,
        "network",
        [
            got, whole(slot), whole(drive), whole(w_hidden), whole(w_out.T), whole(biases),
            whole(fine_order), whole(outgoing_local_lists[0]), state_rows,
            ("raw", links), ("raw", part), ("raw", forcing),
        ],
        [
            (all_groups, False), (all_border, False), (all_links, False), near,
            (shape((3, HID, COLS), f32), False), near, near, (shape((LEV, CELLS), bf16), False),
        ],
        scratch=[pltpu.SemaphoreType.DMA((7,))],
        limit=32,
        flops=5 * 10**9,
    )
    adjoint, heat_back, temp, first, second = kernel(
        second_kernel,
        "second",
        [first, second, border, part, late_forcing, links, ahead],
        [near, near, near, (side, False), (side, False)],
        limit=32,
    )
    first, second = swap(first, second)
    part, ahead = kernel(
        between_kernel, "between", [adjoint, temp, heat, links], [near, near], limit=32
    )
    adjoint, back, temp, first, second = kernel(
        third_kernel,
        "third",
        [first, second, border, part, heat_back, links, ahead],
        [near, (shape((LEV, CELLS), bf16), False), near, (side, False), (side, False)],
        limit=32,
    )
    first, second = swap(first, second)
    sens, top, part, ahead = kernel(
        window_kernel,
        "window",
        [
            adjoint, temp, heat, links, slope, back, groups, whole(w_out.T), whole(w_hidden),
            whole(w_in),
        ],
        [
            (shape((FEAT, CELLS), bf16), "raw"), (shape((TOP, CELLS), f32), False), near, near,
        ],
        scratch=[pltpu.VMEM((FEAT - TOP, CELLS), bf16), pltpu.SemaphoreType.DMA],
        limit=32,
        flops=3 * 10**9,
    )
    sens, temp = kernel(
        finish_kernel,
        "finish",
        [first, second, border, part, links, ahead, top, ("raw", sens)],
        [(shape((FEAT, CELLS), bf16), "raw"), (field, True)],
        scratch=[pltpu.VMEM((TOP, CELLS), bf16), pltpu.SemaphoreType.DMA],
        limit=32,
        aliases={7: 0},
    )
    return temp, sens


def solution(mesh):
    return jax.shard_map(
        local,
        mesh=mesh,
        in_specs=(
            P(None, "cells"),
            P(None, "cells"),
            P(None, "cells"),
            P(),
            P(),
            P(),
            P(),
            P("cells", None),
            P("cells", None),
            P(),
            P("cells", None),
            P(None, "cells"),
            P("cells", None, None),
        ),
        out_specs=(P(None, "cells"), P(None, "cells")),
        check_vma=False,
    )
```

```python
import jax
import jax.numpy as jnp
from jax import lax
from jax.experimental import pallas as pl
from jax.experimental.pallas import tpu as pltpu
from jax.sharding import PartitionSpec as P

LEV, FEAT, HID = 90, 540, 256
COLS, CELLS, HALO = 512, 2048, 256
EXT = CELLS + 2 * HALO
DEVS, CAP = 128, 8
SLOTS = DEVS * CAP
KEEP, SPREAD = 0.25, 0.125
TOP = 96
PIECE = 512
OWN = CELLS // PIECE

f32, bf16, i32 = jnp.float32, jnp.bfloat16, jnp.int32
NN = (((1,), (0,)), ((), ()))
NT = (((1,), (1,)), ((), ()))
TN = (((0,), (0,)), ((), ()))


def dot(a, b, dims):
    return lax.dot_general(a, b, dims, preferred_element_type=f32)


def shape(dims, dtype):
    return jax.ShapeDtypeStruct(dims, dtype)


class Fetch:
    def __init__(self, source, ref, sems, rows, start):
        self.ref, self.rows, self.copies, self.done = ref, rows, [], set()
        for i in range(ref.shape[0] // rows):
            part = pl.ds(i * rows, rows)
            origin = source.at[pl.ds(start + i * rows, rows)]
            self.copies.append(pltpu.make_async_copy(origin, ref.at[part], sems.at[i]))

    def order(self):
        return [len(self.copies) - 1, *range(len(self.copies) - 1)]

    def __call__(self):
        for i in range(len(self.copies)):
            self.piece(i)
        return self.ref

    def piece(self, i):
        if i not in self.done:
            self.copies[i].wait()
            self.done.add(i)
        return self.ref.at[pl.ds(i * self.rows, self.rows)]


class Store:
    def __init__(self, target, ref, sem):
        self.ref = ref
        self.copy = pltpu.make_async_copy(ref, target, sem)

    def put(self):
        self.copy.start()


def kernel(body, name, args, outs, limit=48, flops=10**9, scratch=(), aliases=None):
    arrays, in_specs, plan, scratches = [], [], [], []
    for arg in args:
        if isinstance(arg, tuple) and arg[0] == "raw":
            arrays.append(pltpu.with_memory_space_constraint(arg[1], pltpu.HBM))
            in_specs.append(pl.BlockSpec(memory_space=pl.ANY))
            plan.append(None)
        elif isinstance(arg, tuple):
            array, rows, piece, *start = arg
            arrays.append(pltpu.with_memory_space_constraint(array, pltpu.HBM))
            in_specs.append(pl.BlockSpec(memory_space=pl.ANY))
            plan.append((piece, start[0] if start else 0))
            scratches.append(pltpu.VMEM((rows,) + array.shape[1:], array.dtype))
            scratches.append(pltpu.SemaphoreType.DMA((rows // piece,)))
        else:
            arrays.append(arg)
            in_specs.append(pl.BlockSpec(memory_space=pltpu.VMEM))
            plan.append(None)
    out_shapes, out_specs = [], []
    for out, far in outs:
        if far == "raw":
            out_shapes.append(pltpu.HBM(out.shape, out.dtype))
            out_specs.append(pl.BlockSpec(memory_space=pl.ANY))
        elif far:
            out_shapes.append(pltpu.HBM(out.shape, out.dtype))
            out_specs.append(pl.BlockSpec(memory_space=pl.ANY))
            scratches.append(pltpu.VMEM(out.shape, out.dtype))
            scratches.append(pltpu.SemaphoreType.DMA)
        else:
            out_shapes.append(out)
            out_specs.append(pl.BlockSpec(memory_space=pltpu.VMEM))

    def wrapped(*refs):
        ins, results = refs[: len(args)], refs[len(args) : len(args) + len(outs)]
        rest = list(refs[len(args) + len(outs) :])
        operands, targets = [], []
        for ref, how in zip(ins, plan):
            if how is None:
                operands.append(ref)
            else:
                place, sems = rest.pop(0), rest.pop(0)
                operands.append(Fetch(ref, place, sems, *how))
        for last in (False, True):
            for o in operands:
                if isinstance(o, Fetch) and (len(o.copies) > 1) == last:
                    for i in o.order():
                        o.copies[i].start()
        for ref, (out, far) in zip(results, outs):
            if far is True:
                targets.append(Store(ref, rest.pop(0), rest.pop(0)))
            else:
                targets.append(ref)
        body(*operands, *targets, *rest)
        for target in targets:
            if isinstance(target, Store):
                target.copy.wait()

    size = sum(a.size * a.dtype.itemsize for a in arrays)
    size += sum(o.size * o.dtype.itemsize for o, _ in outs)
    return pl.pallas_call(
        wrapped,
        out_shape=tuple(out_shapes),
        in_specs=in_specs,
        out_specs=tuple(out_specs),
        scratch_shapes=scratches + list(scratch),
        input_output_aliases=aliases or {},
        compiler_params=pltpu.CompilerParams(vmem_limit_bytes=limit * 1024 * 1024),
        cost_estimate=pl.CostEstimate(flops=flops, bytes_accessed=size, transcendentals=0),
        name=name,
    )(*arrays)


def whole(array):
    return (array, array.shape[0], array.shape[0])


def row_iota(rows, columns):
    return lax.broadcasted_iota(i32, (rows, columns), 0)


def lane_iota(rows, columns):
    return lax.broadcasted_iota(i32, (rows, columns), 1)


def onehot(mask):
    return jnp.where(mask, 1.0, 0.0).astype(bf16)


def pick_rows(index, block, columns):
    here = jnp.where(index >> 8 == block, index & 255, -1).astype(f32).astype(bf16)
    place = row_iota(256, columns).astype(f32).astype(bf16)
    return jnp.where(place == here, jnp.ones((), bf16), jnp.zeros((), bf16))


def make_groups(order_ref, groups_ref):
    group = order_ref[...] >> 2
    for c in range(8):
        sl = slice(c * 256, (c + 1) * 256)
        for b in range(2):
            groups_ref[b * 256 : (b + 1) * 256, sl] = pick_rows(group[:, sl], b, 256)


def make_border(lists_ref, border_ref):
    even = (lax.axis_index("cells") & 1) == 0
    near = jnp.where(even, lists_ref[1:2, :], lists_ref[0:1, :])
    far = jnp.where(even, lists_ref[0:1, :], lists_ref[1:2, :])
    for b in range(8):
        sl = slice(b * 256, (b + 1) * 256)
        border_ref[sl, :HALO] = pick_rows(near, b, 256)
        border_ref[sl, HALO:] = pick_rows(far, b, 256)


def to_column(row):
    return jnp.broadcast_to(row, (128, row.shape[1])).T[:, :1]


def chunk(i, size):
    return pl.ds(pl.multiple_of(i * size, size), size)


def route_kernel(parent_ref, request_ref, slot_ref):
    parents = parent_ref[...]
    target = parents >> 9
    column = (parents & (COLS - 1)) + 1
    target_column = to_column(target.astype(f32))
    same = (target_column == target.astype(f32)) & (row_iota(COLS, COLS) < lane_iota(COLS, COLS))
    rank = jnp.sum(jnp.where(same, 1.0, 0.0), axis=0, keepdims=True).astype(i32)
    slot_ref.ref[...] = target * CAP + rank
    slot_ref.put()
    owners = onehot(row_iota(DEVS, COLS) == target)
    high, low = (column >> 4).astype(f32), (column & 15).astype(f32)
    lane = row_iota(DEVS, COLS)
    digits = jnp.where(lane == rank, high, jnp.where(lane == rank + CAP, low, 0.0))
    request_ref.ref[...] = dot(owners, digits.astype(bf16), NT).reshape(DEVS, 1, 128)
    request_ref.put()


def prepare_kernel(
    order_ref, state_ref, w_in_ref, traj_ref, bias_ref, rank_ref, count_ref, drive_ref, u_ref, groups
):
    me = lax.axis_index("cells")
    z = dot(traj_ref()[...], w_in_ref()[...], TN) + bias_ref()[0:1, :]
    decay = jnp.exp(-2.0 * jnp.minimum(jnp.abs(z), 30.0))
    mine = jnp.where(lane_iota(1, DEVS) == me, count_ref()[...], 0).astype(f32)
    daylit = rank_ref()[...].astype(f32) < jnp.sum(mine, axis=1, keepdims=True)
    daylit = to_column(jnp.where(daylit, 1.0, 0.0)) > 0.5
    u = jnp.where(z < 0.0, -decay, decay)
    u_ref.ref[...] = jnp.where(daylit, u, 0.0).astype(bf16)
    u_ref.put()
    make_groups(order_ref(), groups)
    mean = (0.25 * dot(state_ref()[...], groups[...], NT)).astype(bf16)
    drive_ref.ref[...] = dot(w_in_ref.ref[...], mean, TN)
    drive_ref.put()


def answer_kernel(request_ref, u_ref, answer_ref, token_ref, whole_ref, sems):
    request = request_ref[...].reshape(DEVS, 128)
    token_ref.ref[...] = request[:1, :]
    token_ref.put()
    digits = request.astype(bf16)
    number = (lane_iota(1, 128) + 1).astype(f32)
    ones = jnp.ones((128, 128), bf16)
    rows, copies = SLOTS // 2, []
    for h in range(2):
        row, lane = row_iota(rows, 128), lane_iota(rows, 128)
        asker = onehot((row >> 3) + h * (DEVS // 2) == lane)
        weight = jnp.where(lane == (row & 7), 16.0, jnp.where(lane == (row & 7) + CAP, 1.0, 0.0))
        wanted = dot((dot(asker, digits, NN) * weight).astype(bf16), ones, NN)
        chosen = [onehot(wanted == number + 128.0 * c) for c in range(COLS // 128)]
        part = slice(h * rows, (h + 1) * rows)
        u = u_ref()[...]
        whole_ref[part, :] = dot(jnp.concatenate(chosen, axis=1), u, NN).astype(bf16)
        window = pl.ds(h * rows, rows)
        copy = pltpu.make_async_copy(whole_ref.at[window], answer_ref.at[window], sems.at[h])
        copy.start()
        copies.append(copy)
    for copy in copies:
        copy.wait()


def build_kernel(
    slots_ref, lists_ref, forcing_ref, state_ref, token_ref,
    links_ref, part_ref, first_ref, second_ref, links, border_ref, sems,
):
    even = (lax.axis_index("cells") & 1) == 0
    slots = slots_ref()[...]
    high = slots >> 8
    high = jnp.where(even & (high >= 8), 17 - high, high)
    low = slots & 255
    times = jnp.zeros((6, CELLS), f32)
    for k in range(6):
        times = times + jnp.where(slots == slots[k : k + 1, :], 1.0, 0.0)
    times = times.astype(bf16)
    forcing = forcing_ref()

    def fill(jb):
        here = jnp.where(high == jb, low, -1).astype(f32).astype(bf16)
        for c in range(8):
            sl = slice(c * 256, (c + 1) * 256)
            place = row_iota(256, 256).astype(f32).astype(bf16)
            count = jnp.zeros((256, 256), bf16)
            for k in range(6):
                count = jnp.where(here[k : k + 1, sl] == place, times[k : k + 1, sl], count)
            links[jb * 256 : (jb + 1) * 256, sl] = count

    def share(jb):
        return SPREAD * dot(forcing[...], links[jb * 256 : (jb + 1) * 256, :], NT)

    def out(jb):
        rows = pl.ds(jb * 256, 256)
        return pltpu.make_async_copy(links.at[rows], links_ref.at[rows], sems.at[jb])

    def consume(jb):
        if jb == 8:
            first_ref.ref[0] = share(jb).astype(bf16)
        elif jb == 9:
            second_ref.ref[0] = share(jb).astype(bf16)
        else:
            sl = slice(jb * 256, (jb + 1) * 256)
            part_ref.ref[:, sl] = KEEP * forcing[:, sl].astype(f32) + share(jb)

    make_border(lists_ref(), border_ref)
    state = state_ref()
    border = dot(state[:LEV, :], border_ref[...], NN)
    first_ref.ref[1] = border[:, :HALO].astype(bf16)
    second_ref.ref[1] = border[:, HALO:].astype(bf16)
    order = (8, 9, *range(8))
    fill(order[0])
    for now, later in zip(order, order[1:] + (None,)):
        if later is not None:
            fill(later)
        consume(now)
        out(now).start()
    first_ref.put()
    second_ref.put()
    part_ref.put()
    for jb in range(10):
        out(jb).wait()


def received(first, second, border):
    return dot(first, border[:, :HALO], NT) + dot(second, border[:, HALO:], NT)


def push(rounded, links, first_ref, second_ref):
    share = SPREAD * dot(rounded, links[CELLS:, :], NT)
    first_ref[0] = share[:, :HALO].astype(bf16)
    second_ref[0] = share[:, HALO:].astype(bf16)


def pull(adjoint_ref, links, part_ref):
    rounded = adjoint_ref[...].astype(bf16)
    for i in range(OWN):
        sl = slice(i * PIECE, (i + 1) * PIECE)
        part_ref[:, sl] = KEEP * adjoint_ref[:, sl] + SPREAD * dot(rounded, links[sl, :], NT)


def send_border(temp, border, first_ref, second_ref):
    values = dot(temp.astype(bf16), border[...], NN)
    first_ref[1] = values[:, :HALO].astype(bf16)
    second_ref[1] = values[:, HALO:].astype(bf16)


def network_kernel(
    answer_ref, slot_ref, drive_ref, w_hidden_ref, w_out_ref, bias_ref, order_ref, lists_ref,
    state_ref, links_far, part_far, forcing_far,
    groups, border, links, heat_ref, slope_ref, ahead_ref, part_ref, forcing_ref,
    sems,
):
    def piece(i):
        rows = pl.ds(i * PIECE, PIECE)
        return pltpu.make_async_copy(links_far.at[rows], links.at[rows], sems.at[i])

    later = [
        pltpu.make_async_copy(part_far, part_ref, sems.at[OWN + 1]),
        pltpu.make_async_copy(forcing_far, forcing_ref, sems.at[OWN + 2]),
    ]
    small = (slot_ref, drive_ref, w_hidden_ref, w_out_ref, bias_ref, order_ref, lists_ref, state_ref)
    for operand in small:
        operand()
    for i in range(OWN + 1):
        piece(i).start()
    for copy in later:
        copy.start()

    make_groups(order_ref(), groups)
    make_border(lists_ref(), border)
    slots = slot_ref()[...]
    chosen = jnp.concatenate([pick_rows(slots, b, COLS) for b in range(SLOTS // 256)], axis=0)
    u = dot(answer_ref[...], chosen, TN)
    size = jnp.abs(u)
    inverse = 1.0 / (1.0 + size)
    act = jnp.where(u < 0.0, size - 1.0, 1.0 - size) * inverse
    slope = 4.0 * size * inverse * inverse
    slope_ref[0] = slope
    tangent = (slope * drive_ref()[...]).astype(bf16)
    weights, biases = w_hidden_ref(), bias_ref()
    for layer in range(2):
        weight = weights[layer]
        bias = to_column(biases[layer + 1 : layer + 2, :])
        act = jnp.tanh(dot(weight, act.astype(bf16), TN) + bias)
        slope = 1.0 - act * act
        slope_ref[layer + 1] = slope
        tangent = (slope * dot(weight, tangent, TN)).astype(bf16)
    heating = dot(w_out_ref()[...], tangent, NN).astype(bf16)
    heat_ref[...] = dot(heating, groups[...], NN)
    state = state_ref()
    ahead_ref[...] = KEEP * state[:LEV, :].astype(f32) + heat_ref[...]
    for i in range(OWN):
        piece(i).wait()
        sl = slice(i * PIECE, (i + 1) * PIECE)
        ahead_ref[...] += SPREAD * dot(state[:LEV, sl], links[sl, :], NN)
    piece(OWN).wait()
    for copy in later:
        copy.wait()


def second_kernel(
    first_in, second_in, border, part_in, forcing_ref, links, ahead_ref,
    adjoint_ref, heat_back_ref, temp_ref, first_ref, second_ref,
):
    adjoint = part_in[...] + received(first_in[0], second_in[0], border)
    adjoint_ref[...] = adjoint
    push(adjoint.astype(bf16), links, first_ref, second_ref)
    temp = outer(ahead_ref, first_in[1], second_in[1], links)
    temp_ref[...] = temp
    send_border(temp, border, first_ref, second_ref)
    heat_back_ref[...] = forcing_ref[...].astype(f32) + adjoint


def inner(temp_ref, heat_ref, links, part_ref):
    rounded = temp_ref[:LEV, :].astype(bf16)
    for i in range(OWN):
        sl = slice(i * PIECE, (i + 1) * PIECE)
        part_ref[:, sl] = (
            KEEP * temp_ref[:LEV, sl].astype(f32)
            + heat_ref[:, sl]
            + SPREAD * dot(rounded, links[:CELLS, sl], NN)
        )


def outer(part_ref, first, second, links):
    sides = jnp.concatenate([first, second], axis=1)
    return part_ref[...] + SPREAD * dot(sides, links[CELLS:, :], NN)


def between_kernel(adjoint_ref, temp_ref, heat_ref, links, part_ref, ahead_ref):
    pull(adjoint_ref, links, part_ref)
    inner(temp_ref, heat_ref, links, ahead_ref)


def third_kernel(
    first_in, second_in, border, part_in, heat_back_ref, links, ahead_ref,
    adjoint_ref, back_ref, temp_ref, first_ref, second_ref,
):
    adjoint = part_in[...] + received(first_in[0], second_in[0], border)
    adjoint_ref[...] = adjoint
    push(adjoint.astype(bf16), links, first_ref, second_ref)
    temp = outer(ahead_ref, first_in[1], second_in[1], links)
    temp_ref[...] = temp
    send_border(temp, border, first_ref, second_ref)
    back_ref[...] = (heat_back_ref[...] + adjoint).astype(bf16)


def window_kernel(
    adjoint_ref, temp_ref, heat_ref, links, slope_ref, back_ref, groups, w_out_ref, w_hidden_ref,
    w_in_ref, sens_far, top_ref, part_ref, ahead_ref, low_ref, sem,
):
    inner(temp_ref, heat_ref, links, ahead_ref)
    inputs = dot(back_ref[...], groups[...], NT).astype(bf16)
    weights = w_hidden_ref()
    back = (slope_ref[2] * dot(w_out_ref()[...], inputs, TN)).astype(bf16)
    back = (slope_ref[1] * dot(weights[1], back, NN)).astype(bf16)
    back = (slope_ref[0] * dot(weights[0], back, NN)).astype(bf16)
    sens = (0.25 * dot(w_in_ref()[...], back, NN)).astype(bf16)
    low_ref[...] = dot(sens[TOP:], groups[...], NN).astype(bf16)
    copy = pltpu.make_async_copy(low_ref, sens_far.at[pl.ds(TOP, FEAT - TOP)], sem)
    copy.start()
    top_ref[...] = dot(sens[:TOP], groups[...], NN)
    pull(adjoint_ref, links, part_ref)
    copy.wait()


def finish_kernel(
    first_in, second_in, border, part_in, links, ahead_ref, top_in, sens_in,
    sens_far, temp_far, top_ref, sem,
):
    temp_far.ref[...] = outer(ahead_ref, first_in[1], second_in[1], links)
    temp_far.put()
    adjoint = part_in[...] + received(first_in[0], second_in[0], border)
    top_ref[:LEV] = (top_in[:LEV] + adjoint).astype(bf16)
    top_ref[LEV:] = top_in[LEV:].astype(bf16)
    copy = pltpu.make_async_copy(top_ref, sens_far.at[pl.ds(0, TOP)], sem)
    copy.start()
    copy.wait()


def local(
    state_deviation, forcing, trajectory, w_in, w_hidden, w_out, biases, fine_order, group_parent,
    daylit_counts, sun_rank, adjacent_source_slots, outgoing_local_lists,
):
    near_pairs = [(i, i ^ 1) for i in range(DEVS)]
    far_pairs = [(i, (i + 1) % DEVS if i % 2 else (i - 1) % DEVS) for i in range(DEVS)]

    def swap(first, second):
        second = lax.ppermute(second, "cells", far_pairs)
        return lax.ppermute(first, "cells", near_pairs), second

    request, slot = kernel(
        route_kernel,
        "route",
        [group_parent],
        [(shape((DEVS, 1, 128), f32), True), (shape((1, COLS), i32), True)],
        flops=10**7,
    )
    asked = lax.all_to_all(request, "cells", 0, 0, tiled=True)

    side = shape((2, LEV, HALO), bf16)
    field = shape((LEV, CELLS), f32)
    all_links, all_border = shape((EXT, CELLS), bf16), shape((CELLS, 2 * HALO), bf16)
    all_groups = shape((COLS, CELLS), bf16)
    state_rows = (state_deviation, TOP, TOP)

    drive, u = kernel(
        prepare_kernel,
        "prepare",
        [
            whole(fine_order), whole(state_deviation), whole(w_in), whole(trajectory), whole(biases),
            whole(sun_rank), whole(daylit_counts.reshape(1, DEVS)),
        ],
        [(shape((HID, COLS), f32), True), (shape((COLS, HID), bf16), True)],
        scratch=[pltpu.VMEM((COLS, CELLS), bf16)],
        flops=2 * 10**9,
    )
    answer, token = kernel(
        answer_kernel,
        "answer",
        [asked, whole(u)],
        [(shape((SLOTS, HID), bf16), "raw"), (shape((1, 128), f32), True)],
        scratch=[
            pltpu.VMEM((SLOTS, HID), bf16),
            pltpu.SemaphoreType.DMA((2,)),
        ],
    )
    got = lax.all_to_all(answer.reshape(DEVS, CAP, HID), "cells", 0, 0, tiled=True)
    got = got.reshape(SLOTS, HID)
    links, part, first, second = kernel(
        build_kernel,
        "build",
        [
            whole(adjacent_source_slots), whole(outgoing_local_lists[0]), whole(forcing), state_rows,
            ("raw", token),
        ],
        [(all_links, "raw"), (field, True), (side, True), (side, True)],
        scratch=[
            pltpu.VMEM((EXT, CELLS), bf16),
            pltpu.VMEM((CELLS, 2 * HALO), bf16),
            pltpu.SemaphoreType.DMA((10,)),
        ],
        flops=3 * 10**9,
    )
    first, second = swap(first, second)

    near = (field, False)
    groups, border, links, heat, slope, ahead, part, late_forcing = kernel(
        network_kernel,
        "network",
        [
            got, whole(slot), whole(drive), whole(w_hidden), whole(w_out.T), whole(biases),
            whole(fine_order), whole(outgoing_local_lists[0]), state_rows,
            ("raw", links), ("raw", part), ("raw", forcing),
        ],
        [
            (all_groups, False), (all_border, False), (all_links, False), near,
            (shape((3, HID, COLS), f32), False), near, near, (shape((LEV, CELLS), bf16), False),
        ],
        scratch=[pltpu.SemaphoreType.DMA((7,))],
        limit=32,
        flops=5 * 10**9,
    )
    adjoint, heat_back, temp, first, second = kernel(
        second_kernel,
        "second",
        [first, second, border, part, late_forcing, links, ahead],
        [near, near, near, (side, False), (side, False)],
        limit=32,
    )
    first, second = swap(first, second)
    part, ahead = kernel(
        between_kernel, "between", [adjoint, temp, heat, links], [near, near], limit=32
    )
    adjoint, back, temp, first, second = kernel(
        third_kernel,
        "third",
        [first, second, border, part, heat_back, links, ahead],
        [near, (shape((LEV, CELLS), bf16), False), near, (side, False), (side, False)],
        limit=32,
    )
    first, second = swap(first, second)
    sens, top, part, ahead = kernel(
        window_kernel,
        "window",
        [
            adjoint, temp, heat, links, slope, back, groups, whole(w_out.T), whole(w_hidden),
            whole(w_in),
        ],
        [
            (shape((FEAT, CELLS), bf16), "raw"), (shape((TOP, CELLS), f32), False), near, near,
        ],
        scratch=[pltpu.VMEM((FEAT - TOP, CELLS), bf16), pltpu.SemaphoreType.DMA],
        limit=32,
        flops=3 * 10**9,
    )
    sens, temp = kernel(
        finish_kernel,
        "finish",
        [first, second, border, part, links, ahead, top, ("raw", sens)],
        [(shape((FEAT, CELLS), bf16), "raw"), (field, True)],
        scratch=[pltpu.VMEM((TOP, CELLS), bf16), pltpu.SemaphoreType.DMA],
        limit=32,
        aliases={7: 0},
    )
    return temp, sens


def solution(mesh):
    return jax.shard_map(
        local,
        mesh=mesh,
        in_specs=(
            P(None, "cells"),
            P(None, "cells"),
            P(None, "cells"),
            P(),
            P(),
            P(),
            P(),
            P("cells", None),
            P("cells", None),
            P(),
            P("cells", None),
            P(None, "cells"),
            P("cells", None, None),
        ),
        out_specs=(P(None, "cells"), P(None, "cells")),
        check_vma=False,
    )
```

```python
import jax
import jax.numpy as jnp
from jax import lax
from jax.experimental import pallas as pl
from jax.experimental.pallas import tpu as pltpu
from jax.sharding import PartitionSpec as P

LEV, FEAT, HID = 90, 540, 256
COLS, CELLS, HALO = 512, 2048, 256
EXT = CELLS + 2 * HALO
DEVS, CAP = 128, 8
SLOTS = DEVS * CAP
KEEP, SPREAD = 0.25, 0.125
TOP = 96
PIECE = 512
OWN = CELLS // PIECE

f32, bf16, i32 = jnp.float32, jnp.bfloat16, jnp.int32
NN = (((1,), (0,)), ((), ()))
NT = (((1,), (1,)), ((), ()))
TN = (((0,), (0,)), ((), ()))


def dot(a, b, dims):
    return lax.dot_general(a, b, dims, preferred_element_type=f32)


def shape(dims, dtype):
    return jax.ShapeDtypeStruct(dims, dtype)


class Fetch:
    def __init__(self, source, ref, sems, rows, start):
        self.ref, self.rows, self.copies, self.done = ref, rows, [], set()
        for i in range(ref.shape[0] // rows):
            part = pl.ds(i * rows, rows)
            origin = source.at[pl.ds(start + i * rows, rows)]
            self.copies.append(pltpu.make_async_copy(origin, ref.at[part], sems.at[i]))

    def order(self):
        return [len(self.copies) - 1, *range(len(self.copies) - 1)]

    def __call__(self):
        for i in range(len(self.copies)):
            self.piece(i)
        return self.ref

    def piece(self, i):
        if i not in self.done:
            self.copies[i].wait()
            self.done.add(i)
        return self.ref.at[pl.ds(i * self.rows, self.rows)]


class Store:
    def __init__(self, target, ref, sem):
        self.ref = ref
        self.copy = pltpu.make_async_copy(ref, target, sem)

    def put(self):
        self.copy.start()


def kernel(body, name, args, outs, limit=48, flops=10**9, scratch=(), aliases=None):
    arrays, in_specs, plan, scratches = [], [], [], []
    for arg in args:
        if isinstance(arg, tuple) and arg[0] == "raw":
            arrays.append(pltpu.with_memory_space_constraint(arg[1], pltpu.HBM))
            in_specs.append(pl.BlockSpec(memory_space=pl.ANY))
            plan.append(None)
        elif isinstance(arg, tuple):
            array, rows, piece, *start = arg
            arrays.append(pltpu.with_memory_space_constraint(array, pltpu.HBM))
            in_specs.append(pl.BlockSpec(memory_space=pl.ANY))
            plan.append((piece, start[0] if start else 0))
            scratches.append(pltpu.VMEM((rows,) + array.shape[1:], array.dtype))
            scratches.append(pltpu.SemaphoreType.DMA((rows // piece,)))
        else:
            arrays.append(arg)
            in_specs.append(pl.BlockSpec(memory_space=pltpu.VMEM))
            plan.append(None)
    out_shapes, out_specs = [], []
    for out, far in outs:
        if far == "raw":
            out_shapes.append(pltpu.HBM(out.shape, out.dtype))
            out_specs.append(pl.BlockSpec(memory_space=pl.ANY))
        elif far:
            out_shapes.append(pltpu.HBM(out.shape, out.dtype))
            out_specs.append(pl.BlockSpec(memory_space=pl.ANY))
            scratches.append(pltpu.VMEM(out.shape, out.dtype))
            scratches.append(pltpu.SemaphoreType.DMA)
        else:
            out_shapes.append(out)
            out_specs.append(pl.BlockSpec(memory_space=pltpu.VMEM))

    def wrapped(*refs):
        ins, results = refs[: len(args)], refs[len(args) : len(args) + len(outs)]
        rest = list(refs[len(args) + len(outs) :])
        operands, targets = [], []
        for ref, how in zip(ins, plan):
            if how is None:
                operands.append(ref)
            else:
                place, sems = rest.pop(0), rest.pop(0)
                operands.append(Fetch(ref, place, sems, *how))
        for last in (False, True):
            for o in operands:
                if isinstance(o, Fetch) and (len(o.copies) > 1) == last:
                    for i in o.order():
                        o.copies[i].start()
        for ref, (out, far) in zip(results, outs):
            if far is True:
                targets.append(Store(ref, rest.pop(0), rest.pop(0)))
            else:
                targets.append(ref)
        body(*operands, *targets, *rest)
        for target in targets:
            if isinstance(target, Store):
                target.copy.wait()

    size = sum(a.size * a.dtype.itemsize for a in arrays)
    size += sum(o.size * o.dtype.itemsize for o, _ in outs)
    return pl.pallas_call(
        wrapped,
        out_shape=tuple(out_shapes),
        in_specs=in_specs,
        out_specs=tuple(out_specs),
        scratch_shapes=scratches + list(scratch),
        input_output_aliases=aliases or {},
        compiler_params=pltpu.CompilerParams(vmem_limit_bytes=limit * 1024 * 1024),
        cost_estimate=pl.CostEstimate(flops=flops, bytes_accessed=size, transcendentals=0),
        name=name,
    )(*arrays)


def whole(array):
    return (array, array.shape[0], array.shape[0])


def row_iota(rows, columns):
    return lax.broadcasted_iota(i32, (rows, columns), 0)


def lane_iota(rows, columns):
    return lax.broadcasted_iota(i32, (rows, columns), 1)


def onehot(mask):
    return jnp.where(mask, 1.0, 0.0).astype(bf16)


def pick_rows(index, block, columns):
    here = jnp.where(index >> 8 == block, index & 255, -1).astype(f32).astype(bf16)
    place = row_iota(256, columns).astype(f32).astype(bf16)
    return jnp.where(place == here, jnp.ones((), bf16), jnp.zeros((), bf16))


def make_groups(order_ref, groups_ref):
    group = order_ref[...] >> 2
    for c in range(8):
        sl = slice(c * 256, (c + 1) * 256)
        for b in range(2):
            groups_ref[b * 256 : (b + 1) * 256, sl] = pick_rows(group[:, sl], b, 256)


def make_border(lists_ref, border_ref):
    even = (lax.axis_index("cells") & 1) == 0
    near = jnp.where(even, lists_ref[1:2, :], lists_ref[0:1, :])
    far = jnp.where(even, lists_ref[0:1, :], lists_ref[1:2, :])
    for b in range(8):
        sl = slice(b * 256, (b + 1) * 256)
        border_ref[sl, :HALO] = pick_rows(near, b, 256)
        border_ref[sl, HALO:] = pick_rows(far, b, 256)


def to_column(row):
    return jnp.broadcast_to(row, (128, row.shape[1])).T[:, :1]


def chunk(i, size):
    return pl.ds(pl.multiple_of(i * size, size), size)


def route_kernel(parent_ref, request_ref, slot_ref):
    parents = parent_ref()[...]
    target = parents >> 9
    column = (parents & (COLS - 1)) + 1
    target_column = to_column(target.astype(f32))
    same = (target_column == target.astype(f32)) & (row_iota(COLS, COLS) < lane_iota(COLS, COLS))
    rank = jnp.sum(jnp.where(same, 1.0, 0.0), axis=0, keepdims=True).astype(i32)
    slot_ref.ref[...] = target * CAP + rank
    slot_ref.put()
    owners = onehot(row_iota(DEVS, COLS) == target)
    high, low = (column >> 4).astype(f32), (column & 15).astype(f32)
    lane = row_iota(DEVS, COLS)
    digits = jnp.where(lane == rank, high, jnp.where(lane == rank + CAP, low, 0.0))
    request_ref.ref[...] = dot(owners, digits.astype(bf16), NT).reshape(DEVS, 1, 128)
    request_ref.put()


def prepare_kernel(
    order_ref, state_ref, w_in_ref, traj_ref, bias_ref, rank_ref, count_ref, drive_ref, u_ref, groups
):
    me = lax.axis_index("cells")
    z = dot(traj_ref()[...], w_in_ref()[...], TN) + bias_ref()[0:1, :]
    decay = jnp.exp(-2.0 * jnp.minimum(jnp.abs(z), 30.0))
    mine = jnp.where(lane_iota(1, DEVS) == me, count_ref()[...], 0).astype(f32)
    daylit = rank_ref()[...].astype(f32) < jnp.sum(mine, axis=1, keepdims=True)
    daylit = to_column(jnp.where(daylit, 1.0, 0.0)) > 0.5
    u = jnp.where(z < 0.0, -decay, decay)
    u_ref.ref[...] = jnp.where(daylit, u, 0.0).astype(bf16)
    u_ref.put()
    make_groups(order_ref(), groups)
    mean = (0.25 * dot(state_ref()[...], groups[...], NT)).astype(bf16)
    drive_ref.ref[...] = dot(w_in_ref.ref[...], mean, TN)
    drive_ref.put()


def answer_kernel(request_ref, u_ref, answer_ref, token_ref, whole_ref, sems):
    request = request_ref[...].reshape(DEVS, 128)
    token_ref.ref[...] = request[:1, :]
    token_ref.put()
    digits = request.astype(bf16)
    number = (lane_iota(1, 128) + 1).astype(f32)
    ones = jnp.ones((128, 128), bf16)
    rows, copies = SLOTS // 2, []
    for h in range(2):
        row, lane = row_iota(rows, 128), lane_iota(rows, 128)
        asker = onehot((row >> 3) + h * (DEVS // 2) == lane)
        weight = jnp.where(lane == (row & 7), 16.0, jnp.where(lane == (row & 7) + CAP, 1.0, 0.0))
        wanted = dot((dot(asker, digits, NN) * weight).astype(bf16), ones, NN)
        chosen = [onehot(wanted == number + 128.0 * c) for c in range(COLS // 128)]
        part = slice(h * rows, (h + 1) * rows)
        u = u_ref()[...]
        whole_ref[part, :] = dot(jnp.concatenate(chosen, axis=1), u, NN).astype(bf16)
        window = pl.ds(h * rows, rows)
        copy = pltpu.make_async_copy(whole_ref.at[window], answer_ref.at[window], sems.at[h])
        copy.start()
        copies.append(copy)
    for copy in copies:
        copy.wait()


def build_kernel(
    slots_ref, lists_ref, forcing_ref, state_ref, token_ref,
    links_ref, part_ref, first_ref, second_ref, ahead_ref, links, border_ref, sems,
):
    even = (lax.axis_index("cells") & 1) == 0
    slots = slots_ref()[...]
    high = slots >> 8
    high = jnp.where(even & (high >= 8), 17 - high, high)
    low = slots & 255
    times = jnp.zeros((6, CELLS), f32)
    for k in range(6):
        times = times + jnp.where(slots == slots[k : k + 1, :], 1.0, 0.0)
    times = times.astype(bf16)
    forcing = forcing_ref()

    def fill(jb):
        here = jnp.where(high == jb, low, -1).astype(f32).astype(bf16)
        for c in range(8):
            sl = slice(c * 256, (c + 1) * 256)
            place = row_iota(256, 256).astype(f32).astype(bf16)
            count = jnp.zeros((256, 256), bf16)
            for k in range(6):
                count = jnp.where(here[k : k + 1, sl] == place, times[k : k + 1, sl], count)
            links[jb * 256 : (jb + 1) * 256, sl] = count

    def share(jb):
        return SPREAD * dot(forcing[...], links[jb * 256 : (jb + 1) * 256, :], NT)

    def out(jb):
        rows = pl.ds(jb * 256, 256)
        return pltpu.make_async_copy(links.at[rows], links_ref.at[rows], sems.at[jb])

    def consume(jb):
        if jb == 8:
            first_ref.ref[0] = share(jb).astype(bf16)
        elif jb == 9:
            second_ref.ref[0] = share(jb).astype(bf16)
        else:
            sl = slice(jb * 256, (jb + 1) * 256)
            part_ref.ref[:, sl] = KEEP * forcing[:, sl].astype(f32) + share(jb)
            total = SPREAD * dot(state[:LEV, sl], links[sl, :], NN)
            if jb == 0:
                ahead_ref.ref[...] = KEEP * state[:LEV, :].astype(f32) + total
            else:
                ahead_ref.ref[...] += total

    make_border(lists_ref(), border_ref)
    state = state_ref()
    border = dot(state[:LEV, :], border_ref[...], NN)
    first_ref.ref[1] = border[:, :HALO].astype(bf16)
    second_ref.ref[1] = border[:, HALO:].astype(bf16)
    order = (8, 9, *range(8))
    fill(order[0])
    for now, later in zip(order, order[1:] + (None,)):
        if later is not None:
            fill(later)
        consume(now)
        out(now).start()
    first_ref.put()
    second_ref.put()
    part_ref.put()
    ahead_ref.put()
    for jb in range(10):
        out(jb).wait()


def received(first, second, border):
    return dot(first, border[:, :HALO], NT) + dot(second, border[:, HALO:], NT)


def push(rounded, halo, first_ref, second_ref):
    share = SPREAD * dot(rounded, halo[...], NT)
    first_ref[0] = share[:, :HALO].astype(bf16)
    second_ref[0] = share[:, HALO:].astype(bf16)


def pull(adjoint_ref, links, part_ref, wait=None):
    rounded = adjoint_ref[...].astype(bf16)
    for i in range(OWN):
        sl = slice(i * PIECE, (i + 1) * PIECE)
        if wait is not None:
            wait(i)
        part_ref[:, sl] = KEEP * adjoint_ref[:, sl] + SPREAD * dot(rounded, links[sl, :], NT)


def send_border(temp, border, first_ref, second_ref):
    values = dot(temp.astype(bf16), border[...], NN)
    first_ref[1] = values[:, :HALO].astype(bf16)
    second_ref[1] = values[:, HALO:].astype(bf16)


def network_kernel(
    answer_ref, slot_ref, drive_ref, w_hidden_ref, w_out_ref, bias_ref, order_ref, lists_ref,
    own_ref, links_far, part_far, forcing_far,
    groups, border, halo, heat_ref, slope_ref, ahead_ref, part_ref, forcing_ref,
    sems,
):
    later = [
        pltpu.make_async_copy(part_far, part_ref, sems.at[0]),
        pltpu.make_async_copy(forcing_far, forcing_ref, sems.at[1]),
        pltpu.make_async_copy(links_far.at[pl.ds(CELLS, 2 * HALO)], halo, sems.at[2]),
    ]
    small = (slot_ref, drive_ref, w_hidden_ref, w_out_ref, bias_ref, order_ref, lists_ref, own_ref)
    for operand in small:
        operand()
    for copy in later:
        copy.start()

    make_groups(order_ref(), groups)
    make_border(lists_ref(), border)
    slots = slot_ref()[...]
    chosen = jnp.concatenate([pick_rows(slots, b, COLS) for b in range(SLOTS // 256)], axis=0)
    u = dot(answer_ref[...], chosen, TN)
    size = jnp.abs(u)
    inverse = 1.0 / (1.0 + size)
    act = jnp.where(u < 0.0, size - 1.0, 1.0 - size) * inverse
    slope = 4.0 * size * inverse * inverse
    slope_ref[0] = slope
    tangent = (slope * drive_ref()[...]).astype(bf16)
    weights, biases = w_hidden_ref(), bias_ref()
    for layer in range(2):
        weight = weights[layer]
        bias = to_column(biases[layer + 1 : layer + 2, :])
        act = jnp.tanh(dot(weight, act.astype(bf16), TN) + bias)
        slope = 1.0 - act * act
        slope_ref[layer + 1] = slope
        tangent = (slope * dot(weight, tangent, TN)).astype(bf16)
    heating = dot(w_out_ref()[...], tangent, NN).astype(bf16)
    heat = dot(heating, groups[...], NN)
    heat_ref[...] = heat
    ahead_ref[...] = own_ref()[...] + heat
    for copy in later:
        copy.wait()


def second_kernel(
    first_in, second_in, border, part_in, forcing_ref, halo, ahead_ref,
    adjoint_ref, heat_back_ref, temp_ref, first_ref, second_ref,
):
    adjoint = part_in[...] + received(first_in[0], second_in[0], border)
    adjoint_ref[...] = adjoint
    push(adjoint.astype(bf16), halo, first_ref, second_ref)
    temp = outer(ahead_ref, first_in[1], second_in[1], halo)
    temp_ref[...] = temp
    send_border(temp, border, first_ref, second_ref)
    heat_back_ref[...] = forcing_ref[...].astype(f32) + adjoint


def inner(temp_ref, heat_ref, links, part_ref):
    rounded = temp_ref[:LEV, :].astype(bf16)
    for i in range(OWN):
        sl = slice(i * PIECE, (i + 1) * PIECE)
        part_ref[:, sl] = (
            KEEP * temp_ref[:LEV, sl].astype(f32)
            + heat_ref[:, sl]
            + SPREAD * dot(rounded, links[:, sl], NN)
        )


def outer(part_ref, first, second, halo):
    sides = jnp.concatenate([first, second], axis=1)
    return part_ref[...] + SPREAD * dot(sides, halo[...], NN)


def between_kernel(
    adjoint_ref, temp_ref, heat_ref, links_far, links, part_ref, ahead_ref, sems
):
    def piece(i):
        rows = pl.ds(i * PIECE, PIECE)
        return pltpu.make_async_copy(links_far.at[rows], links.at[rows], sems.at[i])

    for i in range(OWN):
        piece(i).start()
    pull(adjoint_ref, links, part_ref, lambda i: piece(i).wait())
    inner(temp_ref, heat_ref, links, ahead_ref)


def third_kernel(
    first_in, second_in, border, part_in, heat_back_ref, halo, ahead_ref,
    adjoint_ref, back_ref, temp_ref, first_ref, second_ref,
):
    adjoint = part_in[...] + received(first_in[0], second_in[0], border)
    adjoint_ref[...] = adjoint
    push(adjoint.astype(bf16), halo, first_ref, second_ref)
    temp = outer(ahead_ref, first_in[1], second_in[1], halo)
    temp_ref[...] = temp
    send_border(temp, border, first_ref, second_ref)
    back_ref[...] = (heat_back_ref[...] + adjoint).astype(bf16)


def window_kernel(
    adjoint_ref, temp_ref, heat_ref, links, slope_ref, back_ref, groups, w_out_ref, w_hidden_ref,
    w_in_ref, sens_far, top_ref, part_ref, ahead_ref, low_ref, sem,
):
    inner(temp_ref, heat_ref, links, ahead_ref)
    inputs = dot(back_ref[...], groups[...], NT).astype(bf16)
    weights = w_hidden_ref()
    back = (slope_ref[2] * dot(w_out_ref()[...], inputs, TN)).astype(bf16)
    back = (slope_ref[1] * dot(weights[1], back, NN)).astype(bf16)
    back = (slope_ref[0] * dot(weights[0], back, NN)).astype(bf16)
    sens = (0.25 * dot(w_in_ref()[...], back, NN)).astype(bf16)
    low_ref[...] = dot(sens[TOP:], groups[...], NN).astype(bf16)
    copy = pltpu.make_async_copy(low_ref, sens_far.at[pl.ds(TOP, FEAT - TOP)], sem)
    copy.start()
    top_ref[...] = dot(sens[:TOP], groups[...], NN)
    pull(adjoint_ref, links, part_ref)
    copy.wait()


def finish_kernel(
    first_in, second_in, border, part_in, halo, ahead_ref, top_in, sens_in,
    sens_far, temp_far, top_ref, sem,
):
    temp_far.ref[...] = outer(ahead_ref, first_in[1], second_in[1], halo)
    temp_far.put()
    adjoint = part_in[...] + received(first_in[0], second_in[0], border)
    top_ref[:LEV] = (top_in[:LEV] + adjoint).astype(bf16)
    top_ref[LEV:] = top_in[LEV:].astype(bf16)
    copy = pltpu.make_async_copy(top_ref, sens_far.at[pl.ds(0, TOP)], sem)
    copy.start()
    copy.wait()


def local(
    state_deviation, forcing, trajectory, w_in, w_hidden, w_out, biases, fine_order, group_parent,
    daylit_counts, sun_rank, adjacent_source_slots, outgoing_local_lists,
):
    near_pairs = [(i, i ^ 1) for i in range(DEVS)]
    far_pairs = [(i, (i + 1) % DEVS if i % 2 else (i - 1) % DEVS) for i in range(DEVS)]

    def swap(first, second):
        second = lax.ppermute(second, "cells", far_pairs)
        return lax.ppermute(first, "cells", near_pairs), second

    request, slot = kernel(
        route_kernel,
        "route",
        [whole(group_parent)],
        [(shape((DEVS, 1, 128), f32), True), (shape((1, COLS), i32), True)],
        flops=10**7,
    )
    asked = lax.all_to_all(request, "cells", 0, 0, tiled=True)

    side = shape((2, LEV, HALO), bf16)
    field = shape((LEV, CELLS), f32)
    all_links, all_border = shape((EXT, CELLS), bf16), shape((CELLS, 2 * HALO), bf16)
    all_groups = shape((COLS, CELLS), bf16)
    state_rows = (state_deviation, TOP, TOP)

    drive, u = kernel(
        prepare_kernel,
        "prepare",
        [
            whole(fine_order), whole(state_deviation), whole(w_in), whole(trajectory), whole(biases),
            whole(sun_rank), whole(daylit_counts.reshape(1, DEVS)),
        ],
        [(shape((HID, COLS), f32), True), (shape((COLS, HID), bf16), True)],
        scratch=[pltpu.VMEM((COLS, CELLS), bf16)],
        flops=2 * 10**9,
    )
    answer, token = kernel(
        answer_kernel,
        "answer",
        [asked, whole(u)],
        [(shape((SLOTS, HID), bf16), "raw"), (shape((1, 128), f32), True)],
        scratch=[
            pltpu.VMEM((SLOTS, HID), bf16),
            pltpu.SemaphoreType.DMA((2,)),
        ],
    )
    got = lax.all_to_all(answer.reshape(DEVS, CAP, HID), "cells", 0, 0, tiled=True)
    got = got.reshape(SLOTS, HID)
    links, part, first, second, own = kernel(
        build_kernel,
        "build",
        [
            whole(adjacent_source_slots), whole(outgoing_local_lists[0]), whole(forcing), state_rows,
            ("raw", token),
        ],
        [(all_links, "raw"), (field, True), (side, True), (side, True), (field, True)],
        scratch=[
            pltpu.VMEM((EXT, CELLS), bf16),
            pltpu.VMEM((CELLS, 2 * HALO), bf16),
            pltpu.SemaphoreType.DMA((10,)),
        ],
        flops=3 * 10**9,
    )
    first, second = swap(first, second)

    near = (field, False)
    groups, border, halo, heat, slope, ahead, part, late_forcing = kernel(
        network_kernel,
        "network",
        [
            got, whole(slot), whole(drive), whole(w_hidden), whole(w_out.T), whole(biases),
            whole(fine_order), whole(outgoing_local_lists[0]), whole(own),
            ("raw", links), ("raw", part), ("raw", forcing),
        ],
        [
            (all_groups, False), (all_border, False), (shape((2 * HALO, CELLS), bf16), False), near,
            (shape((3, HID, COLS), f32), False), near, near, (shape((LEV, CELLS), bf16), False),
        ],
        scratch=[pltpu.SemaphoreType.DMA((3,))],
        limit=32,
        flops=5 * 10**9,
    )
    adjoint, heat_back, temp, first, second = kernel(
        second_kernel,
        "second",
        [first, second, border, part, late_forcing, halo, ahead],
        [near, near, near, (side, False), (side, False)],
        limit=32,
    )
    first, second = swap(first, second)
    links, part, ahead = kernel(
        between_kernel,
        "between",
        [adjoint, temp, heat, ("raw", links)],
        [(shape((CELLS, CELLS), bf16), False), near, near],
        scratch=[pltpu.SemaphoreType.DMA((OWN,))],
        limit=32,
    )
    adjoint, back, temp, first, second = kernel(
        third_kernel,
        "third",
        [first, second, border, part, heat_back, halo, ahead],
        [near, (shape((LEV, CELLS), bf16), False), near, (side, False), (side, False)],
        limit=32,
    )
    first, second = swap(first, second)
    sens, top, part, ahead = kernel(
        window_kernel,
        "window",
        [
            adjoint, temp, heat, links, slope, back, groups, whole(w_out.T), whole(w_hidden),
            whole(w_in),
        ],
        [
            (shape((FEAT, CELLS), bf16), "raw"), (shape((TOP, CELLS), f32), False), near, near,
        ],
        scratch=[pltpu.VMEM((FEAT - TOP, CELLS), bf16), pltpu.SemaphoreType.DMA],
        limit=32,
        flops=3 * 10**9,
    )
    sens, temp = kernel(
        finish_kernel,
        "finish",
        [first, second, border, part, halo, ahead, top, ("raw", sens)],
        [(shape((FEAT, CELLS), bf16), "raw"), (field, True)],
        scratch=[pltpu.VMEM((TOP, CELLS), bf16), pltpu.SemaphoreType.DMA],
        limit=32,
        aliases={7: 0},
    )
    return temp, sens


def solution(mesh):
    return jax.shard_map(
        local,
        mesh=mesh,
        in_specs=(
            P(None, "cells"),
            P(None, "cells"),
            P(None, "cells"),
            P(),
            P(),
            P(),
            P(),
            P("cells", None),
            P("cells", None),
            P(),
            P("cells", None),
            P(None, "cells"),
            P("cells", None, None),
        ),
        out_specs=(P(None, "cells"), P(None, "cells")),
        check_vma=False,
    )
```

```python
import jax
import jax.numpy as jnp
from jax import lax
from jax.experimental import pallas as pl
from jax.experimental.pallas import tpu as pltpu
from jax.sharding import PartitionSpec as P

LEV, FEAT, HID = 90, 540, 256
COLS, CELLS, HALO = 512, 2048, 256
EXT = CELLS + 2 * HALO
DEVS, CAP = 128, 8
SLOTS = DEVS * CAP
KEEP, SPREAD = 0.25, 0.125
TOP = 96
PIECE = 512
OWN = CELLS // PIECE

f32, bf16, i32 = jnp.float32, jnp.bfloat16, jnp.int32
NN = (((1,), (0,)), ((), ()))
NT = (((1,), (1,)), ((), ()))
TN = (((0,), (0,)), ((), ()))


def dot(a, b, dims):
    return lax.dot_general(a, b, dims, preferred_element_type=f32)


def shape(dims, dtype):
    return jax.ShapeDtypeStruct(dims, dtype)


class Fetch:
    def __init__(self, source, ref, sems, rows, start):
        self.ref, self.rows, self.copies, self.done = ref, rows, [], set()
        for i in range(ref.shape[0] // rows):
            part = pl.ds(i * rows, rows)
            origin = source.at[pl.ds(start + i * rows, rows)]
            self.copies.append(pltpu.make_async_copy(origin, ref.at[part], sems.at[i]))

    def order(self):
        return [len(self.copies) - 1, *range(len(self.copies) - 1)]

    def __call__(self):
        for i in range(len(self.copies)):
            self.piece(i)
        return self.ref

    def piece(self, i):
        if i not in self.done:
            self.copies[i].wait()
            self.done.add(i)
        return self.ref.at[pl.ds(i * self.rows, self.rows)]


class Store:
    def __init__(self, target, ref, sem):
        self.ref = ref
        self.copy = pltpu.make_async_copy(ref, target, sem)

    def put(self):
        self.copy.start()


def kernel(body, name, args, outs, limit=48, flops=10**9, scratch=(), aliases=None):
    arrays, in_specs, plan, scratches = [], [], [], []
    for arg in args:
        if isinstance(arg, tuple) and arg[0] == "raw":
            arrays.append(pltpu.with_memory_space_constraint(arg[1], pltpu.HBM))
            in_specs.append(pl.BlockSpec(memory_space=pl.ANY))
            plan.append(None)
        elif isinstance(arg, tuple):
            array, rows, piece, *start = arg
            arrays.append(pltpu.with_memory_space_constraint(array, pltpu.HBM))
            in_specs.append(pl.BlockSpec(memory_space=pl.ANY))
            plan.append((piece, start[0] if start else 0))
            scratches.append(pltpu.VMEM((rows,) + array.shape[1:], array.dtype))
            scratches.append(pltpu.SemaphoreType.DMA((rows // piece,)))
        else:
            arrays.append(arg)
            in_specs.append(pl.BlockSpec(memory_space=pltpu.VMEM))
            plan.append(None)
    out_shapes, out_specs = [], []
    for out, far in outs:
        if far == "raw":
            out_shapes.append(pltpu.HBM(out.shape, out.dtype))
            out_specs.append(pl.BlockSpec(memory_space=pl.ANY))
        elif far:
            out_shapes.append(pltpu.HBM(out.shape, out.dtype))
            out_specs.append(pl.BlockSpec(memory_space=pl.ANY))
            scratches.append(pltpu.VMEM(out.shape, out.dtype))
            scratches.append(pltpu.SemaphoreType.DMA)
        else:
            out_shapes.append(out)
            out_specs.append(pl.BlockSpec(memory_space=pltpu.VMEM))

    def wrapped(*refs):
        ins, results = refs[: len(args)], refs[len(args) : len(args) + len(outs)]
        rest = list(refs[len(args) + len(outs) :])
        operands, targets = [], []
        for ref, how in zip(ins, plan):
            if how is None:
                operands.append(ref)
            else:
                place, sems = rest.pop(0), rest.pop(0)
                operands.append(Fetch(ref, place, sems, *how))
        for last in (False, True):
            for o in operands:
                if isinstance(o, Fetch) and (len(o.copies) > 1) == last:
                    for i in o.order():
                        o.copies[i].start()
        for ref, (out, far) in zip(results, outs):
            if far is True:
                targets.append(Store(ref, rest.pop(0), rest.pop(0)))
            else:
                targets.append(ref)
        body(*operands, *targets, *rest)
        for target in targets:
            if isinstance(target, Store):
                target.copy.wait()

    size = sum(a.size * a.dtype.itemsize for a in arrays)
    size += sum(o.size * o.dtype.itemsize for o, _ in outs)
    return pl.pallas_call(
        wrapped,
        out_shape=tuple(out_shapes),
        in_specs=in_specs,
        out_specs=tuple(out_specs),
        scratch_shapes=scratches + list(scratch),
        input_output_aliases=aliases or {},
        compiler_params=pltpu.CompilerParams(vmem_limit_bytes=limit * 1024 * 1024),
        cost_estimate=pl.CostEstimate(flops=flops, bytes_accessed=size, transcendentals=0),
        name=name,
    )(*arrays)


def whole(array):
    return (array, array.shape[0], array.shape[0])


def row_iota(rows, columns):
    return lax.broadcasted_iota(i32, (rows, columns), 0)


def lane_iota(rows, columns):
    return lax.broadcasted_iota(i32, (rows, columns), 1)


def onehot(mask):
    return jnp.where(mask, 1.0, 0.0).astype(bf16)


def pick_rows(index, block, columns):
    here = jnp.where(index >> 8 == block, index & 255, -1).astype(f32).astype(bf16)
    place = row_iota(256, columns).astype(f32).astype(bf16)
    return jnp.where(place == here, jnp.ones((), bf16), jnp.zeros((), bf16))


def make_groups(order_ref, groups_ref):
    group = order_ref[...] >> 2
    for c in range(8):
        sl = slice(c * 256, (c + 1) * 256)
        for b in range(2):
            groups_ref[b * 256 : (b + 1) * 256, sl] = pick_rows(group[:, sl], b, 256)


def make_border(lists_ref, border_ref):
    even = (lax.axis_index("cells") & 1) == 0
    near = jnp.where(even, lists_ref[1:2, :], lists_ref[0:1, :])
    far = jnp.where(even, lists_ref[0:1, :], lists_ref[1:2, :])
    for b in range(8):
        sl = slice(b * 256, (b + 1) * 256)
        border_ref[sl, :HALO] = pick_rows(near, b, 256)
        border_ref[sl, HALO:] = pick_rows(far, b, 256)


def make_landing(lists_ref, landing_ref):
    even = (lax.axis_index("cells") & 1) == 0
    near = jnp.where(even, lists_ref[1:2, :], lists_ref[0:1, :]).astype(f32)
    far = jnp.where(even, lists_ref[0:1, :], lists_ref[1:2, :]).astype(f32)
    for side, row in enumerate((near, far)):
        cell = to_column(row)
        rows = slice(side * HALO, (side + 1) * HALO)
        for c in range(8):
            lane = (lane_iota(1, 256) + c * 256).astype(f32)
            landing_ref[rows, c * 256 : (c + 1) * 256] = onehot(cell == lane)


def to_column(row):
    return jnp.broadcast_to(row, (128, row.shape[1])).T[:, :1]


def chunk(i, size):
    return pl.ds(pl.multiple_of(i * size, size), size)


def route_kernel(parent_ref, request_ref, slot_ref):
    parents = parent_ref[...]
    target = parents >> 9
    column = (parents & (COLS - 1)) + 1
    target_column = to_column(target.astype(f32))
    same = (target_column == target.astype(f32)) & (row_iota(COLS, COLS) < lane_iota(COLS, COLS))
    rank = jnp.sum(jnp.where(same, 1.0, 0.0), axis=0, keepdims=True).astype(i32)
    slot_ref.ref[...] = target * CAP + rank
    slot_ref.put()
    owners = onehot(row_iota(DEVS, COLS) == target)
    high, low = (column >> 4).astype(f32), (column & 15).astype(f32)
    lane = row_iota(DEVS, COLS)
    digits = jnp.where(lane == rank, high, jnp.where(lane == rank + CAP, low, 0.0))
    request_ref.ref[...] = dot(owners, digits.astype(bf16), NT).reshape(DEVS, 1, 128)
    request_ref.put()


def prepare_kernel(
    order_ref, state_ref, w_in_ref, traj_ref, bias_ref, rank_ref, count_ref, drive_ref, u_ref, groups
):
    me = lax.axis_index("cells")
    z = dot(traj_ref()[...], w_in_ref()[...], TN) + bias_ref()[0:1, :]
    decay = jnp.exp(-2.0 * jnp.minimum(jnp.abs(z), 30.0))
    mine = jnp.where(lane_iota(1, DEVS) == me, count_ref()[...], 0).astype(f32)
    daylit = rank_ref()[...].astype(f32) < jnp.sum(mine, axis=1, keepdims=True)
    daylit = to_column(jnp.where(daylit, 1.0, 0.0)) > 0.5
    u = jnp.where(z < 0.0, -decay, decay)
    u_ref.ref[...] = jnp.where(daylit, u, 0.0).astype(bf16)
    u_ref.put()
    make_groups(order_ref(), groups)
    mean = (0.25 * dot(state_ref()[...], groups[...], NT)).astype(bf16)
    drive_ref.ref[...] = dot(w_in_ref.ref[...], mean, TN)
    drive_ref.put()


def answer_kernel(request_ref, u_ref, answer_ref, token_ref, whole_ref, sems):
    request = request_ref[...].reshape(DEVS, 128)
    token_ref.ref[...] = request[:1, :]
    token_ref.put()
    digits = request.astype(bf16)
    number = (lane_iota(1, 128) + 1).astype(f32)
    ones = jnp.ones((128, 128), bf16)
    rows, copies = SLOTS // 2, []
    for h in range(2):
        row, lane = row_iota(rows, 128), lane_iota(rows, 128)
        asker = onehot((row >> 3) + h * (DEVS // 2) == lane)
        weight = jnp.where(lane == (row & 7), 16.0, jnp.where(lane == (row & 7) + CAP, 1.0, 0.0))
        wanted = dot((dot(asker, digits, NN) * weight).astype(bf16), ones, NN)
        chosen = [onehot(wanted == number + 128.0 * c) for c in range(COLS // 128)]
        part = slice(h * rows, (h + 1) * rows)
        u = u_ref()[...]
        whole_ref[part, :] = dot(jnp.concatenate(chosen, axis=1), u, NN).astype(bf16)
        window = pl.ds(h * rows, rows)
        copy = pltpu.make_async_copy(whole_ref.at[window], answer_ref.at[window], sems.at[h])
        copy.start()
        copies.append(copy)
    for copy in copies:
        copy.wait()


def build_kernel(
    slots_ref, lists_ref, forcing_ref, state_ref, token_ref,
    links_ref, part_ref, first_ref, second_ref, links, border_ref, sems,
):
    even = (lax.axis_index("cells") & 1) == 0
    slots = slots_ref()[...]
    high = slots >> 8
    high = jnp.where(even & (high >= 8), 17 - high, high)
    low = slots & 255
    times = jnp.zeros((6, CELLS), f32)
    for k in range(6):
        times = times + jnp.where(slots == slots[k : k + 1, :], 1.0, 0.0)
    times = times.astype(bf16)
    forcing = forcing_ref()

    def fill(jb):
        here = jnp.where(high == jb, low, -1).astype(f32).astype(bf16)
        for c in range(8):
            sl = slice(c * 256, (c + 1) * 256)
            place = row_iota(256, 256).astype(f32).astype(bf16)
            count = jnp.zeros((256, 256), bf16)
            for k in range(6):
                count = jnp.where(here[k : k + 1, sl] == place, times[k : k + 1, sl], count)
            links[jb * 256 : (jb + 1) * 256, sl] = count

    def share(jb):
        return SPREAD * dot(forcing[...], links[jb * 256 : (jb + 1) * 256, :], NT)

    def out(jb):
        rows = pl.ds(jb * 256, 256)
        return pltpu.make_async_copy(links.at[rows], links_ref.at[rows], sems.at[jb])

    def consume(jb):
        if jb == 8:
            first_ref.ref[0] = share(jb).astype(bf16)
        elif jb == 9:
            second_ref.ref[0] = share(jb).astype(bf16)
        else:
            sl = slice(jb * 256, (jb + 1) * 256)
            part_ref.ref[:, sl] = KEEP * forcing[:, sl].astype(f32) + share(jb)

    make_border(lists_ref(), border_ref)
    state = state_ref()
    border = dot(state[:LEV, :], border_ref[...], NN)
    first_ref.ref[1] = border[:, :HALO].astype(bf16)
    second_ref.ref[1] = border[:, HALO:].astype(bf16)
    order = (8, 9, *range(8))
    fill(order[0])
    for now, later in zip(order, order[1:] + (None,)):
        if later is not None:
            fill(later)
        consume(now)
        out(now).start()
    first_ref.put()
    second_ref.put()
    part_ref.put()
    for jb in range(10):
        out(jb).wait()


def received(first, second, landing):
    return dot(jnp.concatenate([first, second], axis=1), landing[...], NN)


def push(rounded, links, first_ref, second_ref):
    share = SPREAD * dot(rounded, links[CELLS:, :], NT)
    first_ref[0] = share[:, :HALO].astype(bf16)
    second_ref[0] = share[:, HALO:].astype(bf16)


def pull(adjoint_ref, links, part_ref):
    rounded = adjoint_ref[...].astype(bf16)
    for i in range(OWN):
        sl = slice(i * PIECE, (i + 1) * PIECE)
        part_ref[:, sl] = KEEP * adjoint_ref[:, sl] + SPREAD * dot(rounded, links[sl, :], NT)


def send_border(temp, border, first_ref, second_ref):
    values = dot(temp.astype(bf16), border[...], NN)
    first_ref[1] = values[:, :HALO].astype(bf16)
    second_ref[1] = values[:, HALO:].astype(bf16)


def network_kernel(
    answer_ref, slot_ref, drive_ref, w_hidden_ref, w_out_ref, bias_ref, order_ref, lists_ref,
    state_ref, links_far, part_far, forcing_far,
    groups, border, landing, links, heat_ref, slope_ref, ahead_ref, part_ref, forcing_ref,
    sems,
):
    def piece(i):
        rows = pl.ds(i * PIECE, PIECE)
        return pltpu.make_async_copy(links_far.at[rows], links.at[rows], sems.at[i])

    later = [
        pltpu.make_async_copy(part_far, part_ref, sems.at[OWN + 1]),
        pltpu.make_async_copy(forcing_far, forcing_ref, sems.at[OWN + 2]),
    ]
    small = (slot_ref, drive_ref, w_hidden_ref, w_out_ref, bias_ref, order_ref, lists_ref, state_ref)
    for operand in small:
        operand()
    for i in range(OWN + 1):
        piece(i).start()
    for copy in later:
        copy.start()

    make_groups(order_ref(), groups)
    make_border(lists_ref(), border)
    make_landing(lists_ref(), landing)
    slots = slot_ref()[...]
    chosen = jnp.concatenate([pick_rows(slots, b, COLS) for b in range(SLOTS // 256)], axis=0)
    u = dot(answer_ref[...], chosen, TN)
    size = jnp.abs(u)
    inverse = 1.0 / (1.0 + size)
    act = jnp.where(u < 0.0, size - 1.0, 1.0 - size) * inverse
    slope = 4.0 * size * inverse * inverse
    slope_ref[0] = slope
    tangent = (slope * drive_ref()[...]).astype(bf16)
    weights, biases = w_hidden_ref(), bias_ref()
    for layer in range(2):
        weight = weights[layer]
        bias = to_column(biases[layer + 1 : layer + 2, :])
        act = jnp.tanh(dot(weight, act.astype(bf16), TN) + bias)
        slope = 1.0 - act * act
        slope_ref[layer + 1] = slope
        tangent = (slope * dot(weight, tangent, TN)).astype(bf16)
    heating = dot(w_out_ref()[...], tangent, NN).astype(bf16)
    heat_ref[...] = dot(heating, groups[...], NN)
    state = state_ref()
    ahead_ref[...] = KEEP * state[:LEV, :].astype(f32) + heat_ref[...]
    for i in range(OWN):
        piece(i).wait()
        sl = slice(i * PIECE, (i + 1) * PIECE)
        ahead_ref[...] += SPREAD * dot(state[:LEV, sl], links[sl, :], NN)
    piece(OWN).wait()
    for copy in later:
        copy.wait()


def second_kernel(
    first_in, second_in, border, landing, part_in, forcing_ref, links, ahead_ref,
    adjoint_ref, heat_back_ref, temp_ref, first_ref, second_ref,
):
    adjoint = part_in[...] + received(first_in[0], second_in[0], landing)
    adjoint_ref[...] = adjoint
    push(adjoint.astype(bf16), links, first_ref, second_ref)
    temp = outer(ahead_ref, first_in[1], second_in[1], links)
    temp_ref[...] = temp
    send_border(temp, border, first_ref, second_ref)
    heat_back_ref[...] = forcing_ref[...].astype(f32) + adjoint


def inner(temp_ref, heat_ref, links, part_ref):
    rounded = temp_ref[:LEV, :].astype(bf16)
    for i in range(OWN):
        sl = slice(i * PIECE, (i + 1) * PIECE)
        part_ref[:, sl] = (
            KEEP * temp_ref[:LEV, sl].astype(f32)
            + heat_ref[:, sl]
            + SPREAD * dot(rounded, links[:CELLS, sl], NN)
        )


def outer(part_ref, first, second, links):
    sides = jnp.concatenate([first, second], axis=1)
    return part_ref[...] + SPREAD * dot(sides, links[CELLS:, :], NN)


def between_kernel(adjoint_ref, temp_ref, heat_ref, links, part_ref, ahead_ref):
    pull(adjoint_ref, links, part_ref)
    inner(temp_ref, heat_ref, links, ahead_ref)


def third_kernel(
    first_in, second_in, border, landing, part_in, heat_back_ref, links, ahead_ref,
    adjoint_ref, back_ref, temp_ref, first_ref, second_ref,
):
    adjoint = part_in[...] + received(first_in[0], second_in[0], landing)
    adjoint_ref[...] = adjoint
    push(adjoint.astype(bf16), links, first_ref, second_ref)
    temp = outer(ahead_ref, first_in[1], second_in[1], links)
    temp_ref[...] = temp
    send_border(temp, border, first_ref, second_ref)
    back_ref[...] = (heat_back_ref[...] + adjoint).astype(bf16)


def window_kernel(
    adjoint_ref, temp_ref, heat_ref, links, slope_ref, back_ref, groups, w_out_ref, w_hidden_ref,
    w_in_ref, sens_far, top_ref, part_ref, ahead_ref, low_ref, sem,
):
    inner(temp_ref, heat_ref, links, ahead_ref)
    inputs = dot(back_ref[...], groups[...], NT).astype(bf16)
    weights = w_hidden_ref()
    back = (slope_ref[2] * dot(w_out_ref()[...], inputs, TN)).astype(bf16)
    back = (slope_ref[1] * dot(weights[1], back, NN)).astype(bf16)
    back = (slope_ref[0] * dot(weights[0], back, NN)).astype(bf16)
    sens = (0.25 * dot(w_in_ref()[...], back, NN)).astype(bf16)
    low_ref[...] = dot(sens[TOP:], groups[...], NN).astype(bf16)
    copy = pltpu.make_async_copy(low_ref, sens_far.at[pl.ds(TOP, FEAT - TOP)], sem)
    copy.start()
    top_ref[...] = dot(sens[:TOP], groups[...], NN)
    pull(adjoint_ref, links, part_ref)
    copy.wait()


def finish_kernel(
    first_in, second_in, landing, part_in, links, ahead_ref, top_in, sens_in,
    sens_far, temp_far, top_ref, sem,
):
    temp_far.ref[...] = outer(ahead_ref, first_in[1], second_in[1], links)
    temp_far.put()
    adjoint = part_in[...] + received(first_in[0], second_in[0], landing)
    top_ref[:LEV] = (top_in[:LEV] + adjoint).astype(bf16)
    top_ref[LEV:] = top_in[LEV:].astype(bf16)
    copy = pltpu.make_async_copy(top_ref, sens_far.at[pl.ds(0, TOP)], sem)
    copy.start()
    copy.wait()


def local(
    state_deviation, forcing, trajectory, w_in, w_hidden, w_out, biases, fine_order, group_parent,
    daylit_counts, sun_rank, adjacent_source_slots, outgoing_local_lists,
):
    near_pairs = [(i, i ^ 1) for i in range(DEVS)]
    far_pairs = [(i, (i + 1) % DEVS if i % 2 else (i - 1) % DEVS) for i in range(DEVS)]

    def swap(first, second):
        second = lax.ppermute(second, "cells", far_pairs)
        return lax.ppermute(first, "cells", near_pairs), second

    request, slot = kernel(
        route_kernel,
        "route",
        [group_parent],
        [(shape((DEVS, 1, 128), f32), True), (shape((1, COLS), i32), True)],
        flops=10**7,
    )
    asked = lax.all_to_all(request, "cells", 0, 0, tiled=True)

    side = shape((2, LEV, HALO), bf16)
    field = shape((LEV, CELLS), f32)
    all_links, all_border = shape((EXT, CELLS), bf16), shape((CELLS, 2 * HALO), bf16)
    all_groups = shape((COLS, CELLS), bf16)
    state_rows = (state_deviation, TOP, TOP)

    drive, u = kernel(
        prepare_kernel,
        "prepare",
        [
            whole(fine_order), whole(state_deviation), whole(w_in), whole(trajectory), whole(biases),
            whole(sun_rank), whole(daylit_counts.reshape(1, DEVS)),
        ],
        [(shape((HID, COLS), f32), True), (shape((COLS, HID), bf16), True)],
        scratch=[pltpu.VMEM((COLS, CELLS), bf16)],
        flops=2 * 10**9,
    )
    answer, token = kernel(
        answer_kernel,
        "answer",
        [asked, whole(u)],
        [(shape((SLOTS, HID), bf16), "raw"), (shape((1, 128), f32), True)],
        scratch=[
            pltpu.VMEM((SLOTS, HID), bf16),
            pltpu.SemaphoreType.DMA((2,)),
        ],
    )
    got = lax.all_to_all(answer.reshape(DEVS, CAP, HID), "cells", 0, 0, tiled=True)
    got = got.reshape(SLOTS, HID)
    links, part, first, second = kernel(
        build_kernel,
        "build",
        [
            whole(adjacent_source_slots), whole(outgoing_local_lists[0]), whole(forcing), state_rows,
            ("raw", token),
        ],
        [(all_links, "raw"), (field, True), (side, True), (side, True)],
        scratch=[
            pltpu.VMEM((EXT, CELLS), bf16),
            pltpu.VMEM((CELLS, 2 * HALO), bf16),
            pltpu.SemaphoreType.DMA((10,)),
        ],
        flops=3 * 10**9,
    )
    first, second = swap(first, second)

    near = (field, False)
    groups, border, landing, links, heat, slope, ahead, part, late_forcing = kernel(
        network_kernel,
        "network",
        [
            got, whole(slot), whole(drive), whole(w_hidden), whole(w_out.T), whole(biases),
            whole(fine_order), whole(outgoing_local_lists[0]), state_rows,
            ("raw", links), ("raw", part), ("raw", forcing),
        ],
        [
            (all_groups, False), (all_border, False), (shape((2 * HALO, CELLS), bf16), False),
            (all_links, False), near,
            (shape((3, HID, COLS), f32), False), near, near, (shape((LEV, CELLS), bf16), False),
        ],
        scratch=[pltpu.SemaphoreType.DMA((7,))],
        limit=32,
        flops=5 * 10**9,
    )
    adjoint, heat_back, temp, first, second = kernel(
        second_kernel,
        "second",
        [first, second, border, landing, part, late_forcing, links, ahead],
        [near, near, near, (side, False), (side, False)],
        limit=32,
    )
    first, second = swap(first, second)
    part, ahead = kernel(
        between_kernel, "between", [adjoint, temp, heat, links], [near, near], limit=32
    )
    adjoint, back, temp, first, second = kernel(
        third_kernel,
        "third",
        [first, second, border, landing, part, heat_back, links, ahead],
        [near, (shape((LEV, CELLS), bf16), False), near, (side, False), (side, False)],
        limit=32,
    )
    first, second = swap(first, second)
    sens, top, part, ahead = kernel(
        window_kernel,
        "window",
        [
            adjoint, temp, heat, links, slope, back, groups, whole(w_out.T), whole(w_hidden),
            whole(w_in),
        ],
        [
            (shape((FEAT, CELLS), bf16), "raw"), (shape((TOP, CELLS), f32), False), near, near,
        ],
        scratch=[pltpu.VMEM((FEAT - TOP, CELLS), bf16), pltpu.SemaphoreType.DMA],
        limit=32,
        flops=3 * 10**9,
    )
    sens, temp = kernel(
        finish_kernel,
        "finish",
        [first, second, landing, part, links, ahead, top, ("raw", sens)],
        [(shape((FEAT, CELLS), bf16), "raw"), (field, True)],
        scratch=[pltpu.VMEM((TOP, CELLS), bf16), pltpu.SemaphoreType.DMA],
        limit=32,
        aliases={7: 0},
    )
    return temp, sens


def solution(mesh):
    return jax.shard_map(
        local,
        mesh=mesh,
        in_specs=(
            P(None, "cells"),
            P(None, "cells"),
            P(None, "cells"),
            P(),
            P(),
            P(),
            P(),
            P("cells", None),
            P("cells", None),
            P(),
            P("cells", None),
            P(None, "cells"),
            P("cells", None, None),
        ),
        out_specs=(P(None, "cells"), P(None, "cells")),
        check_vma=False,
    )
```
